32 devices in a mesh: split: 8 (over y, x, core), shard: 4 (over z).
Axes of the slice: x: 2, y: 2, z: 4, core: 2. Of those that a mesh axis runs over, the one named last changes fastest.
Arguments:
- strain: bfloat16 [3, 4096], P(None, ('split', 'shard')), may hold values from -6 to 6
- basis: bfloat16 [8, 400, 2048], P('split', 'shard'), may hold values from -0.125 to 0.125
- recon: bfloat16 [8, 2, 2048, 400], P('split', None, 'shard'), may hold values from -0.3125 to 0.3125
Outputs:
- snr2: float32 [8, 2048, 2048], P('split', 'shard')
- loudest: float32 [2048], replicated
The draws below stay inside these ranges and needn't reach their ends.
All inputs are finite; a program needn't handle non-finite values.
Results may differ from the reference program's by a relative error of at most 0.0025.
Values may be sent and summed in bfloat16 or wider, within the bound.
A program may use at most 128 MiB of HBM per device.

```python
import jax
import jax.numpy as jnp
from jax import lax

NDET = 3
NBASIS = 400
TAPS = 2048
TOUT = 2048
SAMPLES = 4096
NSPLIT = 8
TEMPLATES = 2048


def levels(stream_key, dims, cuts, low, top_value):
    factor_of, own = 1.0, jax.random.fold_in(stream_key, 6)
    for dim, shards_of in cuts:
        heights = jnp.exp(jax.random.uniform(jax.random.fold_in(own, dim), (shards_of,), jnp.float32, low / len(cuts), top_value / len(cuts)))
        factor_of = factor_of * jnp.repeat(heights, dims[dim] // shards_of).reshape([-1 if axis == dim else 1 for axis in range(len(dims))])
    return factor_of


def normal_values(rng, extent, deviation, most, cuts=(), kind=jnp.bfloat16):
    gain = levels(rng, extent, cuts, -0.22, 0.18) if cuts else 1.0
    values = jax.random.normal(rng, extent, jnp.float32) * deviation * gain
    return jnp.minimum(jnp.maximum(values, -most), most).astype(kind)


def setup_inputs(seed: int = 0) -> dict:
    streams_of = jax.random.split(jax.random.key(seed), 4)
    return {
        "strain": normal_values(streams_of[0], (NDET, SAMPLES), 1.0, 6.0, ((1, 32),)),
        "basis": normal_values(streams_of[1], (NSPLIT, NBASIS, TAPS), TAPS ** -0.5, 0.125, ((0, 8), (1, 4))),
        "recon": normal_values(streams_of[2], (NSPLIT, 2, TEMPLATES, NBASIS), NBASIS ** -0.5, 0.3125, ((0, 8), (2, 4))),
    }


def toeplitz_block(segment, rows, cols):
    width = rows + cols - 1
    turned = jnp.concatenate([segment[rows - 1:], segment[:rows - 1]])
    flat = jnp.broadcast_to(turned, (rows, width)).reshape(-1)[: rows * (width - 1)]
    return flat.reshape(rows, width - 1)[:, :cols]


def filter_series(signal, filters):
    taps = filters.shape[1]
    tout = signal.shape[0] - taps
    tblock = min(512, tout)
    kblock = min(512, taps)
    outputs = []
    for tpos in range(tout // tblock):
        pieces = []
        for kpos in range(taps // kblock):
            begin = tpos * tblock + taps - (kpos + 1) * kblock
            segment = signal[begin:begin + kblock + tblock - 1]
            pieces.append(toeplitz_block(segment, kblock, tblock))
        frame = jnp.concatenate(pieces, axis=0)
        outputs.append(jnp.dot(filters, frame, preferred_element_type=jnp.float32))
    return jnp.concatenate(outputs, axis=1)


def reference(strain, basis, recon):
    scale = 1.0 / (2.0 * NDET)

    def one_split(pair):
        filters, weights = pair
        series = jnp.stack([filter_series(strain[det], filters).astype(jnp.bfloat16) for det in range(NDET)])
        series_wide = series.astype(jnp.float32)
        mblock = min(512, TEMPLATES)
        blocks = []
        for mpos in range(TEMPLATES // mblock):
            part = weights[:, mpos * mblock:(mpos + 1) * mblock].astype(jnp.float32)
            total = jnp.zeros((mblock, TOUT), jnp.float32)
            for det in range(NDET):
                zvals = jnp.einsum("qml,lt->qmt", part, series_wide[det])
                total = total + jnp.sum(zvals * zvals, axis=0)
            blocks.append(total * scale)
        return jnp.concatenate(blocks, axis=0)

    snr2 = lax.map(one_split, (basis, recon))
    loudest = jnp.max(snr2, axis=(0, 1))
    return snr2, loudest
```

```python
import functools

import jax
import jax.numpy as jnp
from jax import lax
from jax.experimental import pallas as pl
from jax.experimental.pallas import tpu as pltpu
from jax.sharding import PartitionSpec as P

MESH = pl.DeviceIdType.MESH
LANES = 128


def kernel(
    nsplit, nshard, nb, pad, chunks, ntile, scale,
    strain_ref, basis_ref, recon_ref,
    snr_ref, loud_ref,
    parts, rows, tiles, held, acc, series, weights, localmax, splitmax, shardmax,
    strain_send, strain_recv, wide_send, wide_recv,
    basis_send, basis_recv, smax_send, smax_recv, hmax_send, hmax_recv,
):
    split = lax.axis_index("split")
    shard = lax.axis_index("shard")
    ndet, width = strain_ref.shape
    taps = basis_ref.shape[1]
    tout = snr_ref.shape[1]
    templ = snr_ref.shape[0]
    ctaps = taps // chunks
    ktiles = taps // LANES
    nrows = (taps + tout) // LANES

    barrier = pltpu.get_barrier_semaphore()
    for off in range(1, nshard):
        pl.semaphore_signal(barrier, inc=1, device_id={"shard": lax.rem(shard + off, nshard)}, device_id_type=MESH)
    for off in range(1, nsplit):
        pl.semaphore_signal(barrier, inc=1, device_id={"split": lax.rem(split + off, nsplit)}, device_id_type=MESH)
    pl.semaphore_wait(barrier, nshard + nsplit - 2)

    parts[split, shard, :ndet] = strain_ref[...].astype(jnp.float32)

    def strain_copy(off):
        return pltpu.make_async_remote_copy(
            src_ref=parts.at[split, shard], dst_ref=parts.at[split, shard],
            send_sem=strain_send.at[off - 1], recv_sem=strain_recv.at[off - 1],
            device_id={"shard": lax.rem(shard + off, nshard)}, device_id_type=MESH)

    def wide_copy(off):
        return pltpu.make_async_remote_copy(
            src_ref=parts.at[split], dst_ref=parts.at[split],
            send_sem=wide_send.at[off - 1], recv_sem=wide_recv.at[off - 1],
            device_id={"split": lax.rem(split + off, nsplit)}, device_id_type=MESH)

    for off in range(1, nshard):
        strain_copy(off).start()

    def chunk_of(ref, chunk):
        return ref.at[:, pl.ds(pl.multiple_of(chunk * ctaps, ctaps), ctaps)]

    def basis_copy(way, block, chunk, own):
        dst = chunk_of(held.at[block], chunk)
        src = chunk_of(basis_ref, chunk) if own else dst
        target = shard + 1 if way == 0 else shard - 1
        return pltpu.make_async_remote_copy(
            src_ref=src, dst_ref=dst,
            send_sem=basis_send.at[way, block, chunk], recv_sem=basis_recv.at[block, chunk],
            device_id={"shard": target}, device_id_type=MESH)

    for chunk in range(chunks):
        @pl.when(shard < nshard - 1)
        def _():
            basis_copy(0, shard, chunk, True).start()

        @pl.when(shard > 0)
        def _():
            basis_copy(1, shard, chunk, True).start()

    lrow = lax.broadcasted_iota(jnp.int32, (nb * nshard, pad * nshard), 0)
    lcol = lax.broadcasted_iota(jnp.int32, (nb * nshard, pad * nshard), 1)
    within = lax.rem(lcol, pad)
    chosen = (lrow == (lcol - within) // pad * nb + within) & (within < nb)
    select = jnp.where(chosen, 1.0, 0.0).astype(jnp.bfloat16)

    @pl.loop(0, 2 * templ // 256)
    def _(part):
        at = pl.ds(pl.multiple_of(part * 256, 256), 256)
        weights[at, :] = jnp.dot(recon_ref[at, :], select, preferred_element_type=jnp.float32).astype(jnp.bfloat16)

    for off in range(1, nshard):
        strain_copy(off).wait_recv()
    for off in range(1, nsplit):
        wide_copy(off).start()

    @pl.loop(0, ndet * nshard * pad // 64)
    def _(part):
        per = nshard * pad // 64
        series[part // per, pl.ds(pl.multiple_of(lax.rem(part, per) * 64, 64), 64), :] = jnp.zeros((64, tout), jnp.bfloat16)

    for off in range(1, nsplit):
        wide_copy(off).wait_recv()

    per = LANES // width
    if per > 1:
        for piece in range(nsplit * nshard):
            rows[piece // per, :, (piece % per) * width : (piece % per + 1) * width] = parts[piece // nshard, piece % nshard]

    def rolled(b):
        if per > 1:
            block = rows[b]
        else:
            block = parts[b // nshard, lax.rem(b, nshard)]
        return tuple(
            pltpu.roll(jnp.broadcast_to(block[d : d + 1, :], (LANES, LANES)), 1, 1, stride=1, stride_axis=0)
            for d in range(ndet))

    above = lax.broadcasted_iota(jnp.int32, (LANES, LANES), 1) > lax.broadcasted_iota(jnp.int32, (LANES, LANES), 0)

    def tile_step(b, last):
        now = rolled(b)
        at = pl.ds(pl.multiple_of((b - 1) * LANES, LANES), LANES)
        for d in range(ndet):
            tiles[d, :, at] = jnp.where(above, now[d], last[d]).astype(jnp.bfloat16)
        return now

    lax.fori_loop(1, nrows, tile_step, rolled(jnp.int32(0)))

    def fir(filters, slot, block, chunk):
        per_det = tout // ntile

        @pl.loop(0, ndet * per_det)
        def _(step):
            det = step // per_det
            begin = lax.rem(step, per_det) * ntile
            frame = jnp.concatenate([
                tiles[det, :, pl.ds(pl.multiple_of(begin + (ktiles - 1 - i) * LANES - chunk * ctaps, LANES), ntile)]
                for i in range(ctaps // LANES)], axis=0)
            at = pl.ds(pl.multiple_of(begin, ntile), ntile)
            total = jnp.dot(filters[...], frame, preferred_element_type=jnp.float32)
            total = jnp.where(chunk > 0, acc[slot, det, :, at], 0.0) + total
            acc[slot, det, :, at] = total
            series[det, pl.ds(pl.multiple_of(block * pad, pad), nb), at] = total.astype(jnp.bfloat16)

    ahead = min(2, chunks)

    @pl.loop(0, ahead)
    def _(chunk):
        fir(chunk_of(basis_ref, chunk), 2, shard, chunk)

    @pl.loop(0, (nshard - 1) * chunks)
    def _(step):
        hop, chunk = step // chunks, lax.rem(step, chunks)
        below, over = shard - 1 - hop, shard + 1 + hop

        @pl.when(below >= 0)
        def _():
            basis_copy(0, below, chunk, False).wait_recv()

            @pl.when(shard < nshard - 1)
            def _():
                basis_copy(0, below, chunk, False).start()

        @pl.when(over < nshard)
        def _():
            basis_copy(1, over, chunk, False).wait_recv()

            @pl.when(shard > 0)
            def _():
                basis_copy(1, over, chunk, False).start()

        @pl.when(step + ahead < chunks)
        def _():
            fir(chunk_of(basis_ref, step + ahead), 2, shard, step + ahead)

        @pl.when(below >= 0)
        def _():
            fir(chunk_of(held.at[below], chunk), 0, below, chunk)

        @pl.when(over < nshard)
        def _():
            fir(chunk_of(held.at[over], chunk), 1, over, chunk)

    rtile = 256

    @pl.loop(0, tout // rtile)
    def _(step):
        at = pl.ds(pl.multiple_of(step * rtile, rtile), rtile)
        total = None
        for det in range(ndet):
            z = jnp.dot(weights[...], series[det, :, at], preferred_element_type=jnp.float32)
            z = z * z
            z = z[:templ] + z[templ:]
            total = z if total is None else total + z
        total = total * scale
        snr_ref[:, at] = total
        top = jnp.max(total, axis=0, keepdims=True)
        for i in range(rtile // LANES):
            localmax[pl.ds(step * (rtile // LANES) + i, 1), :] = top[:, i * LANES : (i + 1) * LANES]

    def smax_copy(off):
        return pltpu.make_async_remote_copy(
            src_ref=localmax, dst_ref=splitmax.at[off - 1],
            send_sem=smax_send.at[off - 1], recv_sem=smax_recv.at[off - 1],
            device_id={"split": lax.rem(split + off, nsplit)}, device_id_type=MESH)

    for off in range(1, nsplit):
        smax_copy(off).start()
    for off in range(1, nsplit):
        smax_copy(off).wait_recv()
    most = localmax[...]
    for off in range(1, nsplit):
        most = jnp.maximum(most, splitmax[off - 1])
    shardmax[nshard - 1] = most

    def hmax_copy(off):
        return pltpu.make_async_remote_copy(
            src_ref=shardmax.at[nshard - 1], dst_ref=shardmax.at[off - 1],
            send_sem=hmax_send.at[off - 1], recv_sem=hmax_recv.at[off - 1],
            device_id={"shard": lax.rem(shard + off, nshard)}, device_id_type=MESH)

    for off in range(1, nshard):
        hmax_copy(off).start()
    for off in range(1, nshard):
        hmax_copy(off).wait_recv()
    for off in range(1, nshard):
        most = jnp.maximum(most, shardmax[off - 1])
    loud_ref[...] = most

    for off in range(1, nshard):
        strain_copy(off).wait_send()
        hmax_copy(off).wait_send()
    for off in range(1, nsplit):
        wide_copy(off).wait_send()
        smax_copy(off).wait_send()

    @pl.loop(0, nshard * chunks)
    def _(step):
        block, chunk = step // chunks, lax.rem(step, chunks)

        @pl.when((block <= shard) & (shard < nshard - 1))
        def _():
            basis_copy(0, block, chunk, False).wait_send()

        @pl.when((block >= shard) & (shard > 0))
        def _():
            basis_copy(1, block, chunk, False).wait_send()


def per_device(nsplit, nshard, strain, basis, recon):
    ndet, width = strain.shape
    _, nb, taps = basis.shape
    _, _, templ, nbasis = recon.shape
    tout = width * nsplit * nshard - taps
    pad = -(-nb // 64) * 64
    chunks = 4
    ntile = 512
    vmem = pl.BlockSpec(memory_space=pltpu.VMEM)
    dma = pltpu.SemaphoreType.DMA
    snr, loud = pl.pallas_call(
        functools.partial(kernel, nsplit, nshard, nb, pad, chunks, ntile, 1.0 / (2.0 * ndet)),
        out_shape=(
            jax.ShapeDtypeStruct((templ, tout), jnp.float32),
            jax.ShapeDtypeStruct((tout // LANES, LANES), jnp.float32),
        ),
        in_specs=[vmem] * 3,
        out_specs=(vmem, vmem),
        scratch_shapes=[
            pltpu.VMEM((nsplit, nshard, 8, width), jnp.float32),
            pltpu.VMEM(((taps + tout) // LANES, 8, LANES), jnp.float32),
            pltpu.VMEM((ndet, LANES, taps + tout - LANES), jnp.bfloat16),
            pltpu.VMEM((nshard, nb, taps), jnp.bfloat16),
            pltpu.VMEM((3, ndet, nb, tout), jnp.float32),
            pltpu.VMEM((ndet, nshard * pad, tout), jnp.bfloat16),
            pltpu.VMEM((2 * templ, nshard * pad), jnp.bfloat16),
            pltpu.VMEM((tout // LANES, LANES), jnp.float32),
            pltpu.VMEM((nsplit - 1, tout // LANES, LANES), jnp.float32),
            pltpu.VMEM((nshard, tout // LANES, LANES), jnp.float32),
            dma((nshard - 1,)), dma((nshard - 1,)),
            dma((nsplit - 1,)), dma((nsplit - 1,)),
            dma((2, nshard, chunks)), dma((nshard, chunks)),
            dma((nsplit - 1,)), dma((nsplit - 1,)),
            dma((nshard - 1,)), dma((nshard - 1,)),
        ],
        compiler_params=pltpu.CompilerParams(
            collective_id=0, has_side_effects=True, vmem_limit_bytes=56 * 1024 * 1024),
    )(strain, basis[0], recon[0].reshape(2 * templ, nbasis))
    return snr[None], loud.reshape(tout)


def solution(mesh):
    return jax.shard_map(
        functools.partial(per_device, mesh.shape["split"], mesh.shape["shard"]),
        mesh=mesh,
        in_specs=(
            P(None, ("split", "shard")),
            P("split", "shard", None),
            P("split", None, "shard", None),
        ),
        out_specs=(P("split", "shard", None), P()),
        check_vma=False,
    )
```

```python
import functools

import jax
import jax.numpy as jnp
from jax import lax
from jax.experimental import pallas as pl
from jax.experimental.pallas import tpu as pltpu
from jax.sharding import PartitionSpec as P

MESH = pl.DeviceIdType.MESH
LANES = 128


def kernel(
    nsplit, nshard, nb, pad, chunks, mtile, scale,
    strain_ref, basis_ref, recon_ref,
    snr_ref, loud_ref,
    parts, rows, tiles, held, pair, acc, series, weights, localmax, splitmax, shardmax,
    strain_send, strain_recv, wide_send, wide_recv,
    basis_send, basis_recv, smax_send, smax_recv, hmax_send, hmax_recv,
):
    split = lax.axis_index("split")
    shard = lax.axis_index("shard")
    ndet, width = strain_ref.shape
    taps = basis_ref.shape[1]
    tout = snr_ref.shape[1]
    templ = snr_ref.shape[0]
    ctaps = taps // chunks
    ktiles = taps // LANES
    nrows = (taps + tout) // LANES

    barrier = pltpu.get_barrier_semaphore()
    for off in range(1, nshard):
        pl.semaphore_signal(barrier, inc=1, device_id={"shard": lax.rem(shard + off, nshard)}, device_id_type=MESH)
    for off in range(1, nsplit):
        pl.semaphore_signal(barrier, inc=1, device_id={"split": lax.rem(split + off, nsplit)}, device_id_type=MESH)
    pl.semaphore_wait(barrier, nshard + nsplit - 2)

    parts[split, shard] = jnp.zeros((8, width), jnp.float32)
    parts[split, shard, :ndet] = strain_ref[...].astype(jnp.float32)

    def strain_copy(off):
        return pltpu.make_async_remote_copy(
            src_ref=parts.at[split, shard], dst_ref=parts.at[split, shard],
            send_sem=strain_send.at[off - 1], recv_sem=strain_recv.at[off - 1],
            device_id={"shard": lax.rem(shard + off, nshard)}, device_id_type=MESH)

    def wide_copy(off):
        return pltpu.make_async_remote_copy(
            src_ref=parts.at[split], dst_ref=parts.at[split],
            send_sem=wide_send.at[off - 1], recv_sem=wide_recv.at[off - 1],
            device_id={"split": lax.rem(split + off, nsplit)}, device_id_type=MESH)

    for off in range(1, nshard):
        strain_copy(off).start()

    def chunk_of(ref, chunk):
        return ref.at[:, pl.ds(pl.multiple_of(chunk * ctaps, ctaps), ctaps)]

    def basis_copy(way, block, chunk, own):
        dst = chunk_of(held.at[block], chunk)
        src = chunk_of(basis_ref, chunk) if own else dst
        target = shard + 1 if way == 0 else shard - 1
        return pltpu.make_async_remote_copy(
            src_ref=src, dst_ref=dst,
            send_sem=basis_send.at[way, block, chunk], recv_sem=basis_recv.at[block, chunk],
            device_id={"shard": target}, device_id_type=MESH)

    for chunk in range(chunks):
        @pl.when(shard < nshard - 1)
        def _():
            basis_copy(0, shard, chunk, True).start()

        @pl.when(shard > 0)
        def _():
            basis_copy(1, shard, chunk, True).start()

    held[shard] = basis_ref[...]
    lrow = lax.broadcasted_iota(jnp.int32, (nb * nshard, pad * nshard), 0)
    lcol = lax.broadcasted_iota(jnp.int32, (nb * nshard, pad * nshard), 1)
    within = lax.rem(lcol, pad)
    chosen = (lrow == (lcol - within) // pad * nb + within) & (within < nb)
    select = jnp.where(chosen, 1.0, 0.0).astype(jnp.bfloat16)
    for q in range(2):
        @pl.loop(0, templ // 256)
        def _(part):
            begin = pl.multiple_of(part * 256, 256)
            placed = lax.dot_general(
                recon_ref[q, :, pl.ds(begin, 256)], select, (((0,), (0,)), ((), ())),
                preferred_element_type=jnp.float32)
            weights[pl.ds(pl.multiple_of(q * templ + begin, 256), 256), :] = placed.astype(jnp.bfloat16)
    pair[...] = jnp.zeros_like(pair)

    for off in range(1, nshard):
        strain_copy(off).wait_recv()
    for off in range(1, nsplit):
        wide_copy(off).start()

    for off in range(1, nsplit):
        wide_copy(off).wait_recv()

    per = LANES // width
    if per > 1:
        for piece in range(nsplit * nshard):
            rows[piece // per, :, (piece % per) * width : (piece % per + 1) * width] = parts[piece // nshard, piece % nshard]

    def rolled(b):
        if per > 1:
            block = rows[b]
        else:
            block = parts[b // nshard, lax.rem(b, nshard)]
        return tuple(
            pltpu.roll(jnp.broadcast_to(block[d : d + 1, :], (LANES, LANES)), 1, 1, stride=1, stride_axis=0)
            for d in range(ndet))

    above = lax.broadcasted_iota(jnp.int32, (LANES, LANES), 1) > lax.broadcasted_iota(jnp.int32, (LANES, LANES), 0)

    def tile_step(b, last):
        now = rolled(b)
        at = pl.ds(pl.multiple_of((b - 1) * LANES, LANES), LANES)
        for d in range(ndet):
            tiles[d, at, :] = jnp.where(above, now[d], last[d]).T.astype(jnp.bfloat16)
        return now

    lax.fori_loop(1, nrows, tile_step, rolled(jnp.int32(0)))

    def fir(first, second, chunk):
        at_taps = pl.ds(pl.multiple_of(chunk * ctaps, ctaps), ctaps)
        pair[:nb, :] = held[first, :, at_taps]
        pair[pad : pad + nb, :] = held[second, :, at_taps]
        per_det = tout // mtile

        @pl.loop(0, ndet * per_det)
        def _(step):
            det = step // per_det
            begin = lax.rem(step, per_det) * mtile
            frame = jnp.concatenate([
                tiles[det, pl.ds(pl.multiple_of(begin + (ktiles - 1 - i) * LANES - chunk * ctaps, LANES), mtile), :]
                for i in range(ctaps // LANES)], axis=1)
            at = pl.ds(pl.multiple_of(begin, mtile), mtile)
            total = lax.dot_general(frame, pair[...], (((1,), (1,)), ((), ())), preferred_element_type=jnp.float32)
            total = jnp.where(chunk > 0, acc[det, at, :], 0.0) + total
            acc[det, at, :] = total

            @pl.when(chunk == chunks - 1)
            def _():
                series[det, at, pl.ds(pl.multiple_of(first * pad, pad), pad)] = total[:, :pad].astype(jnp.bfloat16)
                series[det, at, pl.ds(pl.multiple_of(second * pad, pad), pad)] = total[:, pad:].astype(jnp.bfloat16)

    both = jnp.minimum(shard, nshard - 1 - shard)
    upper = shard >= nshard // 2

    def single(hop):
        return jnp.where(upper, shard - 1 - hop, shard + 1 + hop)

    @pl.loop(0, (nshard - 1) * chunks)
    def _(step):
        hop, chunk = step // chunks, lax.rem(step, chunks)
        below, over = shard - 1 - hop, shard + 1 + hop

        @pl.when(below >= 0)
        def _():
            basis_copy(0, below, chunk, False).wait_recv()

            @pl.when(shard < nshard - 1)
            def _():
                basis_copy(0, below, chunk, False).start()

        @pl.when(over < nshard)
        def _():
            basis_copy(1, over, chunk, False).wait_recv()

            @pl.when(shard > 0)
            def _():
                basis_copy(1, over, chunk, False).start()

        late = hop - both

        @pl.when((late < 0) | ((late < nshard - 1 - 2 * both) & (lax.rem(late + 2 * nshard, 2) == 0)))
        def _():
            first = jnp.where(late < 0, below, jnp.where(late == 0, shard, single(hop - 1)))
            second = jnp.where(late < 0, over, single(hop))
            fir(first, second, chunk)

    rtile = 256

    @pl.loop(0, tout // rtile)
    def _(step):
        at = pl.ds(pl.multiple_of(step * rtile, rtile), rtile)
        total = None
        for det in range(ndet):
            z = lax.dot_general(
                weights[...], series[det, at, :], (((1,), (1,)), ((), ())), preferred_element_type=jnp.float32)
            z = z * z
            z = z[:templ] + z[templ:]
            total = z if total is None else total + z
        total = total * scale
        snr_ref[:, at] = total
        top = jnp.max(total, axis=0, keepdims=True)
        for i in range(rtile // LANES):
            localmax[pl.ds(step * (rtile // LANES) + i, 1), :] = top[:, i * LANES : (i + 1) * LANES]

    def smax_copy(off):
        return pltpu.make_async_remote_copy(
            src_ref=localmax, dst_ref=splitmax.at[off - 1],
            send_sem=smax_send.at[off - 1], recv_sem=smax_recv.at[off - 1],
            device_id={"split": lax.rem(split + off, nsplit)}, device_id_type=MESH)

    for off in range(1, nsplit):
        smax_copy(off).start()
    for off in range(1, nsplit):
        smax_copy(off).wait_recv()
    most = localmax[...]
    for off in range(1, nsplit):
        most = jnp.maximum(most, splitmax[off - 1])
    shardmax[nshard - 1] = most

    def hmax_copy(off):
        return pltpu.make_async_remote_copy(
            src_ref=shardmax.at[nshard - 1], dst_ref=shardmax.at[off - 1],
            send_sem=hmax_send.at[off - 1], recv_sem=hmax_recv.at[off - 1],
            device_id={"shard": lax.rem(shard + off, nshard)}, device_id_type=MESH)

    for off in range(1, nshard):
        hmax_copy(off).start()
    for off in range(1, nshard):
        hmax_copy(off).wait_recv()
    for off in range(1, nshard):
        most = jnp.maximum(most, shardmax[off - 1])
    loud_ref[...] = most

    for off in range(1, nshard):
        strain_copy(off).wait_send()
        hmax_copy(off).wait_send()
    for off in range(1, nsplit):
        wide_copy(off).wait_send()
        smax_copy(off).wait_send()

    @pl.loop(0, nshard * chunks)
    def _(step):
        block, chunk = step // chunks, lax.rem(step, chunks)

        @pl.when((block <= shard) & (shard < nshard - 1))
        def _():
            basis_copy(0, block, chunk, False).wait_send()

        @pl.when((block >= shard) & (shard > 0))
        def _():
            basis_copy(1, block, chunk, False).wait_send()


def per_device(nsplit, nshard, strain, basis, recon):
    ndet, width = strain.shape
    _, nb, taps = basis.shape
    templ = recon.shape[2]
    tout = width * nsplit * nshard - taps
    pad = -(-nb // LANES) * LANES
    chunks = 4
    mtile = 1024
    vmem = pl.BlockSpec(memory_space=pltpu.VMEM)
    dma = pltpu.SemaphoreType.DMA
    snr, loud = pl.pallas_call(
        functools.partial(kernel, nsplit, nshard, nb, pad, chunks, mtile, 1.0 / (2.0 * ndet)),
        out_shape=(
            pltpu.VMEM((templ, tout), jnp.float32),
            jax.ShapeDtypeStruct((tout // LANES, LANES), jnp.float32),
        ),
        in_specs=[vmem] * 3,
        out_specs=(vmem, vmem),
        scratch_shapes=[
            pltpu.VMEM((nsplit, nshard, 8, width), jnp.float32),
            pltpu.VMEM(((taps + tout) // LANES, 8, LANES), jnp.float32),
            pltpu.VMEM((ndet, taps + tout - LANES, LANES), jnp.bfloat16),
            pltpu.VMEM((nshard, nb, taps), jnp.bfloat16),
            pltpu.VMEM((2 * pad, taps // chunks), jnp.bfloat16),
            pltpu.VMEM((ndet, tout, 2 * pad), jnp.float32),
            pltpu.VMEM((ndet, tout, nshard * pad), jnp.bfloat16),
            pltpu.VMEM((2 * templ, nshard * pad), jnp.bfloat16),
            pltpu.VMEM((tout // LANES, LANES), jnp.float32),
            pltpu.VMEM((nsplit - 1, tout // LANES, LANES), jnp.float32),
            pltpu.VMEM((nshard, tout // LANES, LANES), jnp.float32),
            dma((nshard - 1,)), dma((nshard - 1,)),
            dma((nsplit - 1,)), dma((nsplit - 1,)),
            dma((2, nshard, chunks)), dma((nshard, chunks)),
            dma((nsplit - 1,)), dma((nsplit - 1,)),
            dma((nshard - 1,)), dma((nshard - 1,)),
        ],
        compiler_params=pltpu.CompilerParams(
            collective_id=0, has_side_effects=True, vmem_limit_bytes=56 * 1024 * 1024),
    )(strain, basis[0], jnp.swapaxes(recon[0], 1, 2))
    return snr[None], loud.reshape(tout)


def solution(mesh):
    return jax.shard_map(
        functools.partial(per_device, mesh.shape["split"], mesh.shape["shard"]),
        mesh=mesh,
        in_specs=(
            P(None, ("split", "shard")),
            P("split", "shard", None),
            P("split", None, "shard", None),
        ),
        out_specs=(P("split", "shard", None), P()),
        check_vma=False,
    )
```

```python
import functools

import jax
import jax.numpy as jnp
from jax import lax
from jax.experimental import pallas as pl
from jax.experimental.pallas import tpu as pltpu
from jax.sharding import PartitionSpec as P

MESH = pl.DeviceIdType.MESH
LANES = 128


def kernel(
    nsplit, nshard, nb, pad, chunks, mtile, scale,
    strain_ref, basis_ref, recon_ref,
    snr_ref, loud_ref,
    parts, rows, tiles, held, pair, acc, series, weights, localmax, splitmax, shardmax,
    strain_send, strain_recv, wide_send, wide_recv,
    basis_send, basis_recv, smax_send, smax_recv, hmax_send, hmax_recv,
):
    split = lax.axis_index("split")
    shard = lax.axis_index("shard")
    ndet, width = strain_ref.shape
    taps = basis_ref.shape[1]
    tout = snr_ref.shape[1]
    templ = snr_ref.shape[0]
    ctaps = taps // chunks
    ktiles = taps // LANES
    nrows = (taps + tout) // LANES

    barrier = pltpu.get_barrier_semaphore()
    for off in range(1, nshard):
        pl.semaphore_signal(barrier, inc=1, device_id={"shard": lax.rem(shard + off, nshard)}, device_id_type=MESH)
    for off in range(1, nsplit):
        pl.semaphore_signal(barrier, inc=1, device_id={"split": lax.rem(split + off, nsplit)}, device_id_type=MESH)
    pl.semaphore_wait(barrier, nshard + nsplit - 2)

    parts[split, shard] = jnp.zeros((8, width), jnp.float32)
    parts[split, shard, :ndet] = strain_ref[...].astype(jnp.float32)

    def strain_copy(off):
        return pltpu.make_async_remote_copy(
            src_ref=parts.at[split, shard], dst_ref=parts.at[split, shard],
            send_sem=strain_send.at[off - 1], recv_sem=strain_recv.at[off - 1],
            device_id={"shard": lax.rem(shard + off, nshard)}, device_id_type=MESH)

    def wide_copy(off):
        return pltpu.make_async_remote_copy(
            src_ref=parts.at[split], dst_ref=parts.at[split],
            send_sem=wide_send.at[off - 1], recv_sem=wide_recv.at[off - 1],
            device_id={"split": lax.rem(split + off, nsplit)}, device_id_type=MESH)

    for off in range(1, nshard):
        strain_copy(off).start()

    def chunk_of(ref, chunk):
        return ref.at[:, pl.ds(pl.multiple_of(chunk * ctaps, ctaps), ctaps)]

    def basis_copy(way, block, chunk, own):
        dst = chunk_of(held.at[block], chunk)
        src = chunk_of(basis_ref, chunk) if own else dst
        target = shard + 1 if way == 0 else shard - 1
        return pltpu.make_async_remote_copy(
            src_ref=src, dst_ref=dst,
            send_sem=basis_send.at[way, block, chunk], recv_sem=basis_recv.at[block, chunk],
            device_id={"shard": target}, device_id_type=MESH)

    for chunk in range(chunks):
        @pl.when(shard < nshard - 1)
        def _():
            basis_copy(0, shard, chunk, True).start()

        @pl.when(shard > 0)
        def _():
            basis_copy(1, shard, chunk, True).start()

    held[shard] = basis_ref[...]
    lrow = lax.broadcasted_iota(jnp.int32, (nb * nshard, pad * nshard), 0)
    lcol = lax.broadcasted_iota(jnp.int32, (nb * nshard, pad * nshard), 1)
    within = lax.rem(lcol, pad)
    chosen = (lrow == (lcol - within) // pad * nb + within) & (within < nb)
    select = jnp.where(chosen, 1.0, 0.0).astype(jnp.bfloat16)
    for q in range(2):
        @pl.loop(0, templ // 256)
        def _(part):
            begin = pl.multiple_of(part * 256, 256)
            placed = lax.dot_general(
                recon_ref[q, :, pl.ds(begin, 256)], select, (((0,), (0,)), ((), ())),
                preferred_element_type=jnp.float32)
            weights[pl.ds(pl.multiple_of(q * templ + begin, 256), 256), :] = placed.astype(jnp.bfloat16)
    pair[...] = jnp.zeros_like(pair)

    for off in range(1, nshard):
        strain_copy(off).wait_recv()
    for off in range(1, nsplit):
        wide_copy(off).start()

    for off in range(1, nsplit):
        wide_copy(off).wait_recv()

    steps = (nshard - 1) * chunks
    middle = (shard > 0) & (shard < nshard - 1)
    ahead = chunks - 1
    lead = jnp.where(middle, ahead, 0)

    def advance(step):
        hop, chunk = step // chunks, lax.rem(step, chunks)
        below, over = shard - 1 - hop, shard + 1 + hop

        @pl.when(below >= 0)
        def _():
            basis_copy(0, below, chunk, False).wait_recv()

            @pl.when(shard < nshard - 1)
            def _():
                basis_copy(0, below, chunk, False).start()

        @pl.when(over < nshard)
        def _():
            basis_copy(1, over, chunk, False).wait_recv()

            @pl.when(shard > 0)
            def _():
                basis_copy(1, over, chunk, False).start()

    @pl.when(middle)
    def _():
        for step in range(ahead - 1):
            advance(jnp.int32(step))

    per = LANES // width
    if per > 1:
        for piece in range(nsplit * nshard):
            rows[piece // per, :, (piece % per) * width : (piece % per + 1) * width] = parts[piece // nshard, piece % nshard]

    def rolled(b):
        if per > 1:
            block = rows[b]
        else:
            block = parts[b // nshard, lax.rem(b, nshard)]
        return tuple(
            pltpu.roll(jnp.broadcast_to(block[d : d + 1, :], (LANES, LANES)), 1, 1, stride=1, stride_axis=0)
            for d in range(ndet))

    above = lax.broadcasted_iota(jnp.int32, (LANES, LANES), 1) > lax.broadcasted_iota(jnp.int32, (LANES, LANES), 0)

    def tile_step(b, last):
        now = rolled(b)
        at = pl.ds(pl.multiple_of((b - 1) * LANES, LANES), LANES)
        for d in range(ndet):
            tiles[d, at, :] = jnp.where(above, now[d], last[d]).T.astype(jnp.bfloat16)
        return now

    lax.fori_loop(1, nrows, tile_step, rolled(jnp.int32(0)))

    @pl.when(middle)
    def _():
        advance(jnp.int32(ahead - 1))

    def fir(first, second, chunk):
        at_taps = pl.ds(pl.multiple_of(chunk * ctaps, ctaps), ctaps)
        pair[:nb, :] = held[first, :, at_taps]
        pair[pad : pad + nb, :] = held[second, :, at_taps]
        per_det = tout // mtile

        @pl.loop(0, ndet * per_det)
        def _(step):
            det = step // per_det
            begin = lax.rem(step, per_det) * mtile
            frame = jnp.concatenate([
                tiles[det, pl.ds(pl.multiple_of(begin + (ktiles - 1 - i) * LANES - chunk * ctaps, LANES), mtile), :]
                for i in range(ctaps // LANES)], axis=1)
            at = pl.ds(pl.multiple_of(begin, mtile), mtile)
            total = lax.dot_general(frame, pair[...], (((1,), (1,)), ((), ())), preferred_element_type=jnp.float32)
            total = jnp.where(chunk > 0, acc[det, at, :], 0.0) + total
            acc[det, at, :] = total

            @pl.when(chunk == chunks - 1)
            def _():
                series[det, at, pl.ds(pl.multiple_of(first * pad, pad), pad)] = total[:, :pad].astype(jnp.bfloat16)
                series[det, at, pl.ds(pl.multiple_of(second * pad, pad), pad)] = total[:, pad:].astype(jnp.bfloat16)

    both = jnp.minimum(shard, nshard - 1 - shard)
    upper = shard >= nshard // 2

    def single(hop):
        return jnp.where(upper, shard - 1 - hop, shard + 1 + hop)

    @pl.loop(0, steps)
    def _(step):
        @pl.when(step + lead < steps)
        def _():
            advance(step + lead)

        hop, chunk = step // chunks, lax.rem(step, chunks)
        below, over = shard - 1 - hop, shard + 1 + hop
        late = hop - both

        @pl.when((late < 0) | ((late < nshard - 1 - 2 * both) & (lax.rem(late + 2 * nshard, 2) == 0)))
        def _():
            first = jnp.where(late < 0, below, jnp.where(late == 0, shard, single(hop - 1)))
            second = jnp.where(late < 0, over, single(hop))
            fir(first, second, chunk)

    rtile = 256

    @pl.loop(0, tout // rtile)
    def _(step):
        at = pl.ds(pl.multiple_of(step * rtile, rtile), rtile)
        total = None
        for det in range(ndet):
            z = lax.dot_general(
                weights[...], series[det, at, :], (((1,), (1,)), ((), ())), preferred_element_type=jnp.float32)
            z = z * z
            z = z[:templ] + z[templ:]
            total = z if total is None else total + z
        total = total * scale
        snr_ref[:, at] = total
        top = jnp.max(total, axis=0, keepdims=True)
        for i in range(rtile // LANES):
            localmax[pl.ds(step * (rtile // LANES) + i, 1), :] = top[:, i * LANES : (i + 1) * LANES]

    def smax_copy(off):
        return pltpu.make_async_remote_copy(
            src_ref=localmax, dst_ref=splitmax.at[off - 1],
            send_sem=smax_send.at[off - 1], recv_sem=smax_recv.at[off - 1],
            device_id={"split": lax.rem(split + off, nsplit)}, device_id_type=MESH)

    for off in range(1, nsplit):
        smax_copy(off).start()
    for off in range(1, nsplit):
        smax_copy(off).wait_recv()
    most = localmax[...]
    for off in range(1, nsplit):
        most = jnp.maximum(most, splitmax[off - 1])
    shardmax[nshard - 1] = most

    def hmax_copy(off):
        return pltpu.make_async_remote_copy(
            src_ref=shardmax.at[nshard - 1], dst_ref=shardmax.at[off - 1],
            send_sem=hmax_send.at[off - 1], recv_sem=hmax_recv.at[off - 1],
            device_id={"shard": lax.rem(shard + off, nshard)}, device_id_type=MESH)

    for off in range(1, nshard):
        hmax_copy(off).start()
    for off in range(1, nshard):
        hmax_copy(off).wait_recv()
    for off in range(1, nshard):
        most = jnp.maximum(most, shardmax[off - 1])
    loud_ref[...] = most

    for off in range(1, nshard):
        strain_copy(off).wait_send()
        hmax_copy(off).wait_send()
    for off in range(1, nsplit):
        wide_copy(off).wait_send()
        smax_copy(off).wait_send()

    @pl.loop(0, nshard * chunks)
    def _(step):
        block, chunk = step // chunks, lax.rem(step, chunks)

        @pl.when((block <= shard) & (shard < nshard - 1))
        def _():
            basis_copy(0, block, chunk, False).wait_send()

        @pl.when((block >= shard) & (shard > 0))
        def _():
            basis_copy(1, block, chunk, False).wait_send()


def per_device(nsplit, nshard, strain, basis, recon):
    ndet, width = strain.shape
    _, nb, taps = basis.shape
    templ = recon.shape[2]
    tout = width * nsplit * nshard - taps
    pad = -(-nb // LANES) * LANES
    chunks = 4
    mtile = 1024
    vmem = pl.BlockSpec(memory_space=pltpu.VMEM)
    dma = pltpu.SemaphoreType.DMA
    snr, loud = pl.pallas_call(
        functools.partial(kernel, nsplit, nshard, nb, pad, chunks, mtile, 1.0 / (2.0 * ndet)),
        out_shape=(
            pltpu.VMEM((templ, tout), jnp.float32),
            jax.ShapeDtypeStruct((tout // LANES, LANES), jnp.float32),
        ),
        in_specs=[vmem] * 3,
        out_specs=(vmem, vmem),
        scratch_shapes=[
            pltpu.VMEM((nsplit, nshard, 8, width), jnp.float32),
            pltpu.VMEM(((taps + tout) // LANES, 8, LANES), jnp.float32),
            pltpu.VMEM((ndet, taps + tout - LANES, LANES), jnp.bfloat16),
            pltpu.VMEM((nshard, nb, taps), jnp.bfloat16),
            pltpu.VMEM((2 * pad, taps // chunks), jnp.bfloat16),
            pltpu.VMEM((ndet, tout, 2 * pad), jnp.float32),
            pltpu.VMEM((ndet, tout, nshard * pad), jnp.bfloat16),
            pltpu.VMEM((2 * templ, nshard * pad), jnp.bfloat16),
            pltpu.VMEM((tout // LANES, LANES), jnp.float32),
            pltpu.VMEM((nsplit - 1, tout // LANES, LANES), jnp.float32),
            pltpu.VMEM((nshard, tout // LANES, LANES), jnp.float32),
            dma((nshard - 1,)), dma((nshard - 1,)),
            dma((nsplit - 1,)), dma((nsplit - 1,)),
            dma((2, nshard, chunks)), dma((nshard, chunks)),
            dma((nsplit - 1,)), dma((nsplit - 1,)),
            dma((nshard - 1,)), dma((nshard - 1,)),
        ],
        compiler_params=pltpu.CompilerParams(
            collective_id=0, has_side_effects=True, vmem_limit_bytes=56 * 1024 * 1024),
    )(strain, basis[0], jnp.swapaxes(recon[0], 1, 2))
    return snr[None], loud.reshape(tout)


def solution(mesh):
    return jax.shard_map(
        functools.partial(per_device, mesh.shape["split"], mesh.shape["shard"]),
        mesh=mesh,
        in_specs=(
            P(None, ("split", "shard")),
            P("split", "shard", None),
            P("split", None, "shard", None),
        ),
        out_specs=(P("split", "shard", None), P()),
        check_vma=False,
    )
```

```python
import functools

import jax
import jax.numpy as jnp
from jax import lax
from jax.experimental import pallas as pl
from jax.experimental.pallas import tpu as pltpu
from jax.sharding import PartitionSpec as P

MESH = pl.DeviceIdType.MESH
LANES = 128


def kernel(
    nsplit, nshard, nb, pad, chunks, mtile, scale,
    strain_ref, basis_ref, recon_ref,
    snr_ref, loud_ref,
    parts, rows, tiles, held, pair, turned, acc, series, weights, localmax, splitmax, shardmax,
    strain_send, strain_recv, wide_send, wide_recv,
    basis_send, basis_recv, smax_send, smax_recv, hmax_send, hmax_recv,
):
    split = lax.axis_index("split")
    shard = lax.axis_index("shard")
    ndet, width = strain_ref.shape
    taps = basis_ref.shape[1]
    tout = snr_ref.shape[1]
    templ = snr_ref.shape[0]
    ctaps = taps // chunks
    ktiles = taps // LANES
    nrows = (taps + tout) // LANES

    barrier = pltpu.get_barrier_semaphore()
    for off in range(1, nshard):
        pl.semaphore_signal(barrier, inc=1, device_id={"shard": lax.rem(shard + off, nshard)}, device_id_type=MESH)
    for off in range(1, nsplit):
        pl.semaphore_signal(barrier, inc=1, device_id={"split": lax.rem(split + off, nsplit)}, device_id_type=MESH)
    pl.semaphore_wait(barrier, nshard + nsplit - 2)

    parts[split, shard] = jnp.zeros((8, width), jnp.float32)
    parts[split, shard, :ndet] = strain_ref[...].astype(jnp.float32)

    def strain_copy(off):
        return pltpu.make_async_remote_copy(
            src_ref=parts.at[split, shard], dst_ref=parts.at[split, shard],
            send_sem=strain_send.at[off - 1], recv_sem=strain_recv.at[off - 1],
            device_id={"shard": lax.rem(shard + off, nshard)}, device_id_type=MESH)

    def wide_copy(off):
        return pltpu.make_async_remote_copy(
            src_ref=parts.at[split], dst_ref=parts.at[split],
            send_sem=wide_send.at[off - 1], recv_sem=wide_recv.at[off - 1],
            device_id={"split": lax.rem(split + off, nsplit)}, device_id_type=MESH)

    for off in range(1, nshard):
        strain_copy(off).start()

    def chunk_of(ref, chunk):
        return ref.at[:, pl.ds(pl.multiple_of(chunk * ctaps, ctaps), ctaps)]

    def basis_copy(way, block, chunk, own):
        dst = chunk_of(held.at[block], chunk)
        src = chunk_of(basis_ref, chunk) if own else dst
        target = shard + 1 if way == 0 else shard - 1
        return pltpu.make_async_remote_copy(
            src_ref=src, dst_ref=dst,
            send_sem=basis_send.at[way, block, chunk], recv_sem=basis_recv.at[block, chunk],
            device_id={"shard": target}, device_id_type=MESH)

    for chunk in range(chunks):
        @pl.when(shard < nshard - 1)
        def _():
            basis_copy(0, shard, chunk, True).start()

        @pl.when(shard > 0)
        def _():
            basis_copy(1, shard, chunk, True).start()

    held[shard] = basis_ref[...]
    lrow = lax.broadcasted_iota(jnp.int32, (nb * nshard, pad * nshard), 0)
    lcol = lax.broadcasted_iota(jnp.int32, (nb * nshard, pad * nshard), 1)
    within = lax.rem(lcol, pad)
    chosen = (lrow == (lcol - within) // pad * nb + within) & (within < nb)
    select = jnp.where(chosen, 1.0, 0.0).astype(jnp.bfloat16)
    for q in range(2):
        @pl.loop(0, templ // 256)
        def _(part):
            begin = pl.multiple_of(part * 256, 256)
            placed = lax.dot_general(
                recon_ref[q, :, pl.ds(begin, 256)], select, (((0,), (0,)), ((), ())),
                preferred_element_type=jnp.float32)
            weights[pl.ds(pl.multiple_of(q * templ + begin, 256), 256), :] = placed.astype(jnp.bfloat16)
    pair[...] = jnp.zeros_like(pair)

    for off in range(1, nshard):
        strain_copy(off).wait_recv()
    for off in range(1, nsplit):
        wide_copy(off).start()

    for off in range(1, nsplit):
        wide_copy(off).wait_recv()

    middle = (shard > 0) & (shard < nshard - 1)
    ahead = min(2, chunks)

    def advance(step):
        hop, chunk = step // chunks, lax.rem(step, chunks)
        below, over = shard - 1 - hop, shard + 1 + hop

        @pl.when(below >= 0)
        def _():
            basis_copy(0, below, chunk, False).wait_recv()

            @pl.when(shard < nshard - 1)
            def _():
                basis_copy(0, below, chunk, False).start()

        @pl.when(over < nshard)
        def _():
            basis_copy(1, over, chunk, False).wait_recv()

            @pl.when(shard > 0)
            def _():
                basis_copy(1, over, chunk, False).start()

    @pl.when(middle)
    def _():
        for step in range(ahead):
            advance(jnp.int32(step))

    per = LANES // width
    if per > 1:
        for piece in range(nsplit * nshard):
            rows[piece // per, :, (piece % per) * width : (piece % per + 1) * width] = parts[piece // nshard, piece % nshard]

    def rolled(b):
        if per > 1:
            block = rows[b]
        else:
            block = parts[b // nshard, lax.rem(b, nshard)]
        return tuple(
            pltpu.roll(jnp.broadcast_to(block[d : d + 1, :], (LANES, LANES)), 1, 1, stride=1, stride_axis=0)
            for d in range(ndet))

    above = lax.broadcasted_iota(jnp.int32, (LANES, LANES), 1) > lax.broadcasted_iota(jnp.int32, (LANES, LANES), 0)

    def tile_step(b, last):
        now = rolled(b)
        at = pl.ds(pl.multiple_of((b - 1) * LANES, LANES), LANES)
        for d in range(ndet):
            tiles[d, at, :] = jnp.where(above, now[d], last[d]).T.astype(jnp.bfloat16)
        return now

    lax.fori_loop(1, nrows, tile_step, rolled(jnp.int32(0)))

    @pl.loop(jnp.where(middle, ahead, 0), chunks)
    def _(step):
        advance(step)

    def place(first, second, chunk):
        at_taps = pl.ds(pl.multiple_of(chunk * ctaps, ctaps), ctaps)
        pair[:nb, :] = held[first, :, at_taps]
        pair[pad : pad + nb, :] = held[second, :, at_taps]
        turned[at_taps, :] = pair[...].T

    def keep(det, at, first, second, total):
        series[det, at, pl.ds(pl.multiple_of(first * pad, pad), pad)] = total[:, :pad].astype(jnp.bfloat16)
        series[det, at, pl.ds(pl.multiple_of(second * pad, pad), pad)] = total[:, pad:].astype(jnp.bfloat16)

    per_det = tout // mtile

    def fir_whole(first, second, beside):
        @pl.loop(0, chunks)
        def _(chunk):
            place(first, second, chunk)

        @pl.loop(0, ndet * per_det)
        def _(step):
            det = step // per_det
            begin = lax.rem(step, per_det) * mtile
            frame = jnp.concatenate([
                tiles[det, pl.ds(pl.multiple_of(begin + (ktiles - 1 - i) * LANES, LANES), mtile), :]
                for i in range(ktiles)], axis=1)
            at = pl.ds(pl.multiple_of(begin, mtile), mtile)
            keep(det, at, first, second, jnp.dot(frame, turned[...], preferred_element_type=jnp.float32))
            beside(step)

    def fir_part(first, second, chunk):
        place(first, second, chunk)
        at_taps = pl.ds(pl.multiple_of(chunk * ctaps, ctaps), ctaps)

        @pl.loop(0, ndet * per_det)
        def _(step):
            det = step // per_det
            begin = lax.rem(step, per_det) * mtile
            frame = jnp.concatenate([
                tiles[det, pl.ds(pl.multiple_of(begin + (ktiles - 1 - i) * LANES - chunk * ctaps, LANES), mtile), :]
                for i in range(ctaps // LANES)], axis=1)
            at = pl.ds(pl.multiple_of(begin, mtile), mtile)
            total = jnp.dot(frame, turned[at_taps, :], preferred_element_type=jnp.float32)
            total = jnp.where(chunk > 0, acc[det, at, :], 0.0) + total

            @pl.when(chunk < chunks - 1)
            def _():
                acc[det, at, :] = total

            @pl.when(chunk == chunks - 1)
            def _():
                keep(det, at, first, second, total)

    both = jnp.minimum(shard, nshard - 1 - shard)
    upper = shard >= nshard // 2

    def single(hop):
        return jnp.where(upper, shard - 1 - hop, shard + 1 + hop)

    @pl.loop(0, nshard - 1)
    def _(hop):
        late = hop - both
        paired = (late < 0) | ((late < nshard - 1 - 2 * both) & (lax.rem(late + 2 * nshard, 2) == 0))
        first = jnp.where(late < 0, shard - 1 - hop, jnp.where(late == 0, shard, single(hop - 1)))
        second = jnp.where(late < 0, shard + 1 + hop, single(hop))
        by_chunk = jnp.logical_not(middle) & (hop == nshard - 2)
        onward = (hop + 1 < nshard - 1) & (middle | (hop + 1 < nshard - 2))

        @pl.when(by_chunk)
        def _():
            @pl.loop(0, chunks)
            def _(chunk):
                @pl.when(hop > 0)
                def _():
                    advance(hop * chunks + chunk)

                fir_part(first, second, chunk)

        def beside(step):
            @pl.when(onward & (step < chunks))
            def _():
                advance((hop + 1) * chunks + step)

        @pl.when(paired & jnp.logical_not(by_chunk))
        def _():
            fir_whole(first, second, beside)

        @pl.when(jnp.logical_not(paired))
        def _():
            @pl.loop(0, chunks)
            def _(step):
                beside(step)

    rtile = 256

    @pl.loop(0, tout // rtile)
    def _(step):
        at = pl.ds(pl.multiple_of(step * rtile, rtile), rtile)
        total = None
        for det in range(ndet):
            z = lax.dot_general(
                weights[...], series[det, at, :], (((1,), (1,)), ((), ())), preferred_element_type=jnp.float32)
            z = z * z
            z = z[:templ] + z[templ:]
            total = z if total is None else total + z
        total = total * scale
        snr_ref[:, at] = total
        top = jnp.max(total, axis=0, keepdims=True)
        for i in range(rtile // LANES):
            localmax[pl.ds(step * (rtile // LANES) + i, 1), :] = top[:, i * LANES : (i + 1) * LANES]

    def smax_copy(off):
        return pltpu.make_async_remote_copy(
            src_ref=localmax, dst_ref=splitmax.at[off - 1],
            send_sem=smax_send.at[off - 1], recv_sem=smax_recv.at[off - 1],
            device_id={"split": lax.rem(split + off, nsplit)}, device_id_type=MESH)

    for off in range(1, nsplit):
        smax_copy(off).start()
    for off in range(1, nsplit):
        smax_copy(off).wait_recv()
    most = localmax[...]
    for off in range(1, nsplit):
        most = jnp.maximum(most, splitmax[off - 1])
    shardmax[nshard - 1] = most

    def hmax_copy(off):
        return pltpu.make_async_remote_copy(
            src_ref=shardmax.at[nshard - 1], dst_ref=shardmax.at[off - 1],
            send_sem=hmax_send.at[off - 1], recv_sem=hmax_recv.at[off - 1],
            device_id={"shard": lax.rem(shard + off, nshard)}, device_id_type=MESH)

    for off in range(1, nshard):
        hmax_copy(off).start()
    for off in range(1, nshard):
        hmax_copy(off).wait_recv()
    for off in range(1, nshard):
        most = jnp.maximum(most, shardmax[off - 1])
    loud_ref[...] = most

    for off in range(1, nshard):
        strain_copy(off).wait_send()
        hmax_copy(off).wait_send()
    for off in range(1, nsplit):
        wide_copy(off).wait_send()
        smax_copy(off).wait_send()

    @pl.loop(0, nshard * chunks)
    def _(step):
        block, chunk = step // chunks, lax.rem(step, chunks)

        @pl.when((block <= shard) & (shard < nshard - 1))
        def _():
            basis_copy(0, block, chunk, False).wait_send()

        @pl.when((block >= shard) & (shard > 0))
        def _():
            basis_copy(1, block, chunk, False).wait_send()


def per_device(nsplit, nshard, strain, basis, recon):
    ndet, width = strain.shape
    _, nb, taps = basis.shape
    templ = recon.shape[2]
    tout = width * nsplit * nshard - taps
    pad = -(-nb // LANES) * LANES
    chunks = 4
    mtile = 1024
    vmem = pl.BlockSpec(memory_space=pltpu.VMEM)
    dma = pltpu.SemaphoreType.DMA
    snr, loud = pl.pallas_call(
        functools.partial(kernel, nsplit, nshard, nb, pad, chunks, mtile, 1.0 / (2.0 * ndet)),
        out_shape=(
            pltpu.VMEM((templ, tout), jnp.float32),
            jax.ShapeDtypeStruct((tout // LANES, LANES), jnp.float32),
        ),
        in_specs=[vmem] * 3,
        out_specs=(vmem, vmem),
        scratch_shapes=[
            pltpu.VMEM((nsplit, nshard, 8, width), jnp.float32),
            pltpu.VMEM(((taps + tout) // LANES, 8, LANES), jnp.float32),
            pltpu.VMEM((ndet, taps + tout - LANES, LANES), jnp.bfloat16),
            pltpu.VMEM((nshard, nb, taps), jnp.bfloat16),
            pltpu.VMEM((2 * pad, taps // chunks), jnp.bfloat16),
            pltpu.VMEM((taps, 2 * pad), jnp.bfloat16),
            pltpu.VMEM((ndet, tout, 2 * pad), jnp.float32),
            pltpu.VMEM((ndet, tout, nshard * pad), jnp.bfloat16),
            pltpu.VMEM((2 * templ, nshard * pad), jnp.bfloat16),
            pltpu.VMEM((tout // LANES, LANES), jnp.float32),
            pltpu.VMEM((nsplit - 1, tout // LANES, LANES), jnp.float32),
            pltpu.VMEM((nshard, tout // LANES, LANES), jnp.float32),
            dma((nshard - 1,)), dma((nshard - 1,)),
            dma((nsplit - 1,)), dma((nsplit - 1,)),
            dma((2, nshard, chunks)), dma((nshard, chunks)),
            dma((nsplit - 1,)), dma((nsplit - 1,)),
            dma((nshard - 1,)), dma((nshard - 1,)),
        ],
        compiler_params=pltpu.CompilerParams(
            collective_id=0, has_side_effects=True, vmem_limit_bytes=56 * 1024 * 1024),
    )(strain, basis[0], jnp.swapaxes(recon[0], 1, 2))
    return snr[None], loud.reshape(tout)


def solution(mesh):
    return jax.shard_map(
        functools.partial(per_device, mesh.shape["split"], mesh.shape["shard"]),
        mesh=mesh,
        in_specs=(
            P(None, ("split", "shard")),
            P("split", "shard", None),
            P("split", None, "shard", None),
        ),
        out_specs=(P("split", "shard", None), P()),
        check_vma=False,
    )
```

```python
import functools

import jax
import jax.numpy as jnp
from jax import lax
from jax.experimental import pallas as pl
from jax.experimental.pallas import tpu as pltpu
from jax.sharding import PartitionSpec as P

MESH = pl.DeviceIdType.MESH
LANES = 128


def kernel(
    nsplit, nshard, nb, pad, chunks, mtile, scale,
    strain_ref, basis_ref, recon_ref,
    snr_ref, loud_ref,
    parts, rows, tiles, held, pair, turned, acc, series, partial, weights, localmax, splitmax, shardmax,
    strain_send, strain_recv, wide_send, wide_recv,
    basis_send, basis_recv, smax_send, smax_recv, hmax_send, hmax_recv,
):
    split = lax.axis_index("split")
    shard = lax.axis_index("shard")
    ndet, width = strain_ref.shape
    taps = basis_ref.shape[1]
    tout = snr_ref.shape[1]
    templ = snr_ref.shape[0]
    ctaps = taps // chunks
    ktiles = taps // LANES
    nrows = (taps + tout) // LANES

    barrier = pltpu.get_barrier_semaphore()
    for off in range(1, nshard):
        pl.semaphore_signal(barrier, inc=1, device_id={"shard": lax.rem(shard + off, nshard)}, device_id_type=MESH)
    for off in range(1, nsplit):
        pl.semaphore_signal(barrier, inc=1, device_id={"split": lax.rem(split + off, nsplit)}, device_id_type=MESH)
    pl.semaphore_wait(barrier, nshard + nsplit - 2)

    parts[split, shard] = jnp.zeros((8, width), jnp.float32)
    parts[split, shard, :ndet] = strain_ref[...].astype(jnp.float32)

    def strain_copy(off):
        return pltpu.make_async_remote_copy(
            src_ref=parts.at[split, shard], dst_ref=parts.at[split, shard],
            send_sem=strain_send.at[off - 1], recv_sem=strain_recv.at[off - 1],
            device_id={"shard": lax.rem(shard + off, nshard)}, device_id_type=MESH)

    def wide_copy(off):
        return pltpu.make_async_remote_copy(
            src_ref=parts.at[split], dst_ref=parts.at[split],
            send_sem=wide_send.at[off - 1], recv_sem=wide_recv.at[off - 1],
            device_id={"split": lax.rem(split + off, nsplit)}, device_id_type=MESH)

    for off in range(1, nshard):
        strain_copy(off).start()

    def chunk_of(ref, chunk):
        return ref.at[:, pl.ds(pl.multiple_of(chunk * ctaps, ctaps), ctaps)]

    def basis_copy(way, block, chunk, own):
        dst = chunk_of(held.at[block], chunk)
        src = chunk_of(basis_ref, chunk) if own else dst
        target = shard + 1 if way == 0 else shard - 1
        return pltpu.make_async_remote_copy(
            src_ref=src, dst_ref=dst,
            send_sem=basis_send.at[way, block, chunk], recv_sem=basis_recv.at[block, chunk],
            device_id={"shard": target}, device_id_type=MESH)

    for chunk in range(chunks):
        @pl.when(shard < nshard - 1)
        def _():
            basis_copy(0, shard, chunk, True).start()

        @pl.when(shard > 0)
        def _():
            basis_copy(1, shard, chunk, True).start()

    held[shard] = basis_ref[...]
    lrow = lax.broadcasted_iota(jnp.int32, (nb * nshard, pad * nshard), 0)
    lcol = lax.broadcasted_iota(jnp.int32, (nb * nshard, pad * nshard), 1)
    within = lax.rem(lcol, pad)
    chosen = (lrow == (lcol - within) // pad * nb + within) & (within < nb)
    select = jnp.where(chosen, 1.0, 0.0).astype(jnp.bfloat16)
    for q in range(2):
        @pl.loop(0, templ // 256)
        def _(part):
            begin = pl.multiple_of(part * 256, 256)
            placed = lax.dot_general(
                recon_ref[q, :, pl.ds(begin, 256)], select, (((0,), (0,)), ((), ())),
                preferred_element_type=jnp.float32)
            weights[pl.ds(pl.multiple_of(q * templ + begin, 256), 256), :] = placed.astype(jnp.bfloat16)
    pair[...] = jnp.zeros_like(pair)

    for off in range(1, nshard):
        strain_copy(off).wait_recv()
    for off in range(1, nsplit):
        wide_copy(off).start()

    for off in range(1, nsplit):
        wide_copy(off).wait_recv()

    middle = (shard > 0) & (shard < nshard - 1)
    ahead = min(2, chunks)

    def advance(step):
        hop, chunk = step // chunks, lax.rem(step, chunks)
        below, over = shard - 1 - hop, shard + 1 + hop

        @pl.when(below >= 0)
        def _():
            basis_copy(0, below, chunk, False).wait_recv()

            @pl.when(shard < nshard - 1)
            def _():
                basis_copy(0, below, chunk, False).start()

        @pl.when(over < nshard)
        def _():
            basis_copy(1, over, chunk, False).wait_recv()

            @pl.when(shard > 0)
            def _():
                basis_copy(1, over, chunk, False).start()

    @pl.when(middle)
    def _():
        for step in range(ahead):
            advance(jnp.int32(step))

    per = LANES // width
    if per > 1:
        for piece in range(nsplit * nshard):
            rows[piece // per, :, (piece % per) * width : (piece % per + 1) * width] = parts[piece // nshard, piece % nshard]

    def rolled(b):
        if per > 1:
            block = rows[b]
        else:
            block = parts[b // nshard, lax.rem(b, nshard)]
        return tuple(
            pltpu.roll(jnp.broadcast_to(block[d : d + 1, :], (LANES, LANES)), 1, 1, stride=1, stride_axis=0)
            for d in range(ndet))

    above = lax.broadcasted_iota(jnp.int32, (LANES, LANES), 1) > lax.broadcasted_iota(jnp.int32, (LANES, LANES), 0)

    def tile_step(b, last):
        now = rolled(b)
        at = pl.ds(pl.multiple_of((b - 1) * LANES, LANES), LANES)
        for d in range(ndet):
            tiles[d, at, :] = jnp.where(above, now[d], last[d]).T.astype(jnp.bfloat16)
        return now

    lax.fori_loop(1, nrows, tile_step, rolled(jnp.int32(0)))

    @pl.loop(jnp.where(middle, ahead, 0), chunks)
    def _(step):
        advance(step)

    def place(first, second, chunk):
        at_taps = pl.ds(pl.multiple_of(chunk * ctaps, ctaps), ctaps)
        pair[:nb, :] = held[first, :, at_taps]
        pair[pad : pad + nb, :] = held[second, :, at_taps]
        turned[at_taps, :] = pair[...].T

    rtile = 256

    def columns(block):
        return weights[:, pl.ds(pl.multiple_of(block * pad, pad), pad)]

    def term(first, second, det, at):
        return lax.dot_general(
            jnp.concatenate([columns(first), columns(second)], axis=1), series[det, at, :],
            (((1,), (1,)), ((), ())), preferred_element_type=jnp.float32)

    def add_terms(first, second, begins):
        @pl.loop(0, ndet * (tout // rtile))
        def _(step):
            det = step // (tout // rtile)
            at = pl.ds(pl.multiple_of(lax.rem(step, tout // rtile) * rtile, rtile), rtile)

            @pl.when(begins)
            def _():
                partial[det, :, at] = term(first, second, det, at)

            @pl.when(jnp.logical_not(begins))
            def _():
                partial[det, :, at] += term(first, second, det, at)

    per_det = tout // mtile

    def fir_whole(first, second, beside):
        @pl.loop(0, chunks)
        def _(chunk):
            place(first, second, chunk)

        @pl.loop(0, ndet * per_det)
        def _(step):
            det = step // per_det
            begin = lax.rem(step, per_det) * mtile
            frame = jnp.concatenate([
                tiles[det, pl.ds(pl.multiple_of(begin + (ktiles - 1 - i) * LANES, LANES), mtile), :]
                for i in range(ktiles)], axis=1)
            at = pl.ds(pl.multiple_of(begin, mtile), mtile)
            series[det, at, :] = jnp.dot(frame, turned[...], preferred_element_type=jnp.float32).astype(jnp.bfloat16)
            beside(step)

    def fir_part(first, second, chunk):
        place(first, second, chunk)
        at_taps = pl.ds(pl.multiple_of(chunk * ctaps, ctaps), ctaps)

        @pl.loop(0, ndet * per_det)
        def _(step):
            det = step // per_det
            begin = lax.rem(step, per_det) * mtile
            frame = jnp.concatenate([
                tiles[det, pl.ds(pl.multiple_of(begin + (ktiles - 1 - i) * LANES - chunk * ctaps, LANES), mtile), :]
                for i in range(ctaps // LANES)], axis=1)
            at = pl.ds(pl.multiple_of(begin, mtile), mtile)
            total = jnp.dot(frame, turned[at_taps, :], preferred_element_type=jnp.float32)
            total = jnp.where(chunk > 0, acc[det, at, :], 0.0) + total

            @pl.when(chunk < chunks - 1)
            def _():
                acc[det, at, :] = total

            @pl.when(chunk == chunks - 1)
            def _():
                series[det, at, :] = total.astype(jnp.bfloat16)

    both = jnp.minimum(shard, nshard - 1 - shard)
    upper = shard >= nshard // 2

    def single(hop):
        return jnp.where(upper, shard - 1 - hop, shard + 1 + hop)

    @pl.loop(0, nshard - 1)
    def _(hop):
        late = hop - both
        paired = (late < 0) | ((late < nshard - 1 - 2 * both) & (lax.rem(late + 2 * nshard, 2) == 0))
        first = jnp.where(late < 0, shard - 1 - hop, jnp.where(late == 0, shard, single(hop - 1)))
        second = jnp.where(late < 0, shard + 1 + hop, single(hop))
        by_chunk = jnp.logical_not(middle) & (hop == nshard - 2)

        @pl.when(jnp.logical_not(middle) & (hop > 0) & jnp.logical_not(by_chunk))
        def _():
            @pl.loop(0, chunks)
            def _(step):
                advance(hop * chunks + step)

        @pl.when(by_chunk)
        def _():
            @pl.loop(0, chunks)
            def _(chunk):
                @pl.when(hop > 0)
                def _():
                    advance(hop * chunks + chunk)

                fir_part(first, second, chunk)

        def beside(step):
            @pl.when(middle & (hop + 1 < nshard - 1) & (step < chunks))
            def _():
                advance((hop + 1) * chunks + step)

        @pl.when(paired & jnp.logical_not(by_chunk))
        def _():
            fir_whole(first, second, beside)

            @pl.when(hop < nshard - 2 - both)
            def _():
                add_terms(first, second, hop == 0)

        @pl.when(jnp.logical_not(paired))
        def _():
            @pl.loop(0, chunks)
            def _(step):
                beside(step)

    last = nshard - 2 - both
    first = jnp.where(last == both, shard, single(last - 1))
    second = single(last)

    @pl.loop(0, tout // rtile)
    def _(step):
        at = pl.ds(pl.multiple_of(step * rtile, rtile), rtile)
        total = None
        for det in range(ndet):
            z = partial[det, :, at] + term(first, second, det, at)
            z = z * z
            z = z[:templ] + z[templ:]
            total = z if total is None else total + z
        total = total * scale
        snr_ref[:, at] = total
        top = jnp.max(total, axis=0, keepdims=True)
        for i in range(rtile // LANES):
            localmax[pl.ds(step * (rtile // LANES) + i, 1), :] = top[:, i * LANES : (i + 1) * LANES]

    def smax_copy(off):
        return pltpu.make_async_remote_copy(
            src_ref=localmax, dst_ref=splitmax.at[off - 1],
            send_sem=smax_send.at[off - 1], recv_sem=smax_recv.at[off - 1],
            device_id={"split": lax.rem(split + off, nsplit)}, device_id_type=MESH)

    for off in range(1, nsplit):
        smax_copy(off).start()
    for off in range(1, nsplit):
        smax_copy(off).wait_recv()
    most = localmax[...]
    for off in range(1, nsplit):
        most = jnp.maximum(most, splitmax[off - 1])
    shardmax[nshard - 1] = most

    def hmax_copy(off):
        return pltpu.make_async_remote_copy(
            src_ref=shardmax.at[nshard - 1], dst_ref=shardmax.at[off - 1],
            send_sem=hmax_send.at[off - 1], recv_sem=hmax_recv.at[off - 1],
            device_id={"shard": lax.rem(shard + off, nshard)}, device_id_type=MESH)

    for off in range(1, nshard):
        hmax_copy(off).start()
    for off in range(1, nshard):
        hmax_copy(off).wait_recv()
    for off in range(1, nshard):
        most = jnp.maximum(most, shardmax[off - 1])
    loud_ref[...] = most

    for off in range(1, nshard):
        strain_copy(off).wait_send()
        hmax_copy(off).wait_send()
    for off in range(1, nsplit):
        wide_copy(off).wait_send()
        smax_copy(off).wait_send()

    @pl.loop(0, nshard * chunks)
    def _(step):
        block, chunk = step // chunks, lax.rem(step, chunks)

        @pl.when((block <= shard) & (shard < nshard - 1))
        def _():
            basis_copy(0, block, chunk, False).wait_send()

        @pl.when((block >= shard) & (shard > 0))
        def _():
            basis_copy(1, block, chunk, False).wait_send()


def per_device(nsplit, nshard, strain, basis, recon):
    ndet, width = strain.shape
    _, nb, taps = basis.shape
    templ = recon.shape[2]
    tout = width * nsplit * nshard - taps
    pad = -(-nb // LANES) * LANES
    chunks = 4
    mtile = 1024
    vmem = pl.BlockSpec(memory_space=pltpu.VMEM)
    dma = pltpu.SemaphoreType.DMA
    snr, loud = pl.pallas_call(
        functools.partial(kernel, nsplit, nshard, nb, pad, chunks, mtile, 1.0 / (2.0 * ndet)),
        out_shape=(
            pltpu.VMEM((templ, tout), jnp.float32),
            jax.ShapeDtypeStruct((tout // LANES, LANES), jnp.float32),
        ),
        in_specs=[vmem] * 3,
        out_specs=(vmem, vmem),
        scratch_shapes=[
            pltpu.VMEM((nsplit, nshard, 8, width), jnp.float32),
            pltpu.VMEM(((taps + tout) // LANES, 8, LANES), jnp.float32),
            pltpu.VMEM((ndet, taps + tout - LANES, LANES), jnp.bfloat16),
            pltpu.VMEM((nshard, nb, taps), jnp.bfloat16),
            pltpu.VMEM((2 * pad, taps // chunks), jnp.bfloat16),
            pltpu.VMEM((taps, 2 * pad), jnp.bfloat16),
            pltpu.VMEM((ndet, tout, 2 * pad), jnp.float32),
            pltpu.VMEM((ndet, tout, 2 * pad), jnp.bfloat16),
            pltpu.VMEM((ndet, 2 * templ, tout), jnp.float32),
            pltpu.VMEM((2 * templ, nshard * pad), jnp.bfloat16),
            pltpu.VMEM((tout // LANES, LANES), jnp.float32),
            pltpu.VMEM((nsplit - 1, tout // LANES, LANES), jnp.float32),
            pltpu.VMEM((nshard, tout // LANES, LANES), jnp.float32),
            dma((nshard - 1,)), dma((nshard - 1,)),
            dma((nsplit - 1,)), dma((nsplit - 1,)),
            dma((2, nshard, chunks)), dma((nshard, chunks)),
            dma((nsplit - 1,)), dma((nsplit - 1,)),
            dma((nshard - 1,)), dma((nshard - 1,)),
        ],
        compiler_params=pltpu.CompilerParams(
            collective_id=0, has_side_effects=True, vmem_limit_bytes=56 * 1024 * 1024),
    )(strain, basis[0], jnp.swapaxes(recon[0], 1, 2))
    return snr[None], loud.reshape(tout)


def solution(mesh):
    return jax.shard_map(
        functools.partial(per_device, mesh.shape["split"], mesh.shape["shard"]),
        mesh=mesh,
        in_specs=(
            P(None, ("split", "shard")),
            P("split", "shard", None),
            P("split", None, "shard", None),
        ),
        out_specs=(P("split", "shard", None), P()),
        check_vma=False,
    )
```

```python
import functools

import jax
import jax.numpy as jnp
from jax import lax
from jax.experimental import pallas as pl
from jax.experimental.pallas import tpu as pltpu
from jax.sharding import PartitionSpec as P

MESH = pl.DeviceIdType.MESH
LANES = 128


def kernel(
    nsplit, nshard, nb, pad, chunks, mtile, scale,
    strain_ref, basis_ref, recon_ref,
    snr_ref, loud_ref,
    parts, rows, tiles, held, pair, turned, acc, series, weights, localmax, splitmax, shardmax,
    strain_send, strain_recv, wide_send, wide_recv,
    basis_send, basis_recv, smax_send, smax_recv, hmax_send, hmax_recv,
):
    split = lax.axis_index("split")
    shard = lax.axis_index("shard")
    ndet, width = strain_ref.shape
    taps = basis_ref.shape[1]
    tout = snr_ref.shape[1]
    templ = snr_ref.shape[0]
    ctaps = taps // chunks
    ktiles = taps // LANES
    nrows = (taps + tout) // LANES

    barrier = pltpu.get_barrier_semaphore()
    for off in range(1, nshard):
        pl.semaphore_signal(barrier, inc=1, device_id={"shard": lax.rem(shard + off, nshard)}, device_id_type=MESH)
    for off in range(1, nsplit):
        pl.semaphore_signal(barrier, inc=1, device_id={"split": lax.rem(split + off, nsplit)}, device_id_type=MESH)
    pl.semaphore_wait(barrier, nshard + nsplit - 2)

    parts[split, shard] = jnp.zeros((8, width), jnp.float32)
    parts[split, shard, :ndet] = strain_ref[...].astype(jnp.float32)

    def strain_copy(off):
        return pltpu.make_async_remote_copy(
            src_ref=parts.at[split, shard], dst_ref=parts.at[split, shard],
            send_sem=strain_send.at[off - 1], recv_sem=strain_recv.at[off - 1],
            device_id={"shard": lax.rem(shard + off, nshard)}, device_id_type=MESH)

    def wide_copy(off):
        return pltpu.make_async_remote_copy(
            src_ref=parts.at[split], dst_ref=parts.at[split],
            send_sem=wide_send.at[off - 1], recv_sem=wide_recv.at[off - 1],
            device_id={"split": lax.rem(split + off, nsplit)}, device_id_type=MESH)

    for off in range(1, nshard):
        strain_copy(off).start()

    def chunk_of(ref, chunk):
        return ref.at[:, pl.ds(pl.multiple_of(chunk * ctaps, ctaps), ctaps)]

    def basis_copy(way, block, chunk, own):
        dst = chunk_of(held.at[block], chunk)
        src = chunk_of(basis_ref, chunk) if own else dst
        target = shard + 1 if way == 0 else shard - 1
        return pltpu.make_async_remote_copy(
            src_ref=src, dst_ref=dst,
            send_sem=basis_send.at[way, block, chunk], recv_sem=basis_recv.at[block, chunk],
            device_id={"shard": target}, device_id_type=MESH)

    for chunk in range(chunks):
        @pl.when(shard < nshard - 1)
        def _():
            basis_copy(0, shard, chunk, True).start()

        @pl.when(shard > 0)
        def _():
            basis_copy(1, shard, chunk, True).start()

    held[shard] = basis_ref[...]
    lrow = lax.broadcasted_iota(jnp.int32, (nb * nshard, pad * nshard), 0)
    lcol = lax.broadcasted_iota(jnp.int32, (nb * nshard, pad * nshard), 1)
    within = lax.rem(lcol, pad)
    chosen = (lrow == (lcol - within) // pad * nb + within) & (within < nb)
    select = jnp.where(chosen, 1.0, 0.0).astype(jnp.bfloat16)

    def place_weights(q):
        @pl.loop(0, templ // 256)
        def _(part):
            begin = pl.multiple_of(part * 256, 256)
            placed = lax.dot_general(
                recon_ref[q, :, pl.ds(begin, 256)], select, (((0,), (0,)), ((), ())),
                preferred_element_type=jnp.float32)
            weights[pl.ds(pl.multiple_of(q * templ + begin, 256), 256), :] = placed.astype(jnp.bfloat16)

    place_weights(0)
    pair[...] = jnp.zeros_like(pair)

    for off in range(1, nshard):
        strain_copy(off).wait_recv()
    for off in range(1, nsplit):
        wide_copy(off).start()

    place_weights(1)
    for off in range(1, nsplit):
        wide_copy(off).wait_recv()

    middle = (shard > 0) & (shard < nshard - 1)

    def advance(step):
        hop, chunk = step // chunks, lax.rem(step, chunks)
        below, over = shard - 1 - hop, shard + 1 + hop

        @pl.when(below >= 0)
        def _():
            basis_copy(0, below, chunk, False).wait_recv()

            @pl.when(shard < nshard - 1)
            def _():
                basis_copy(0, below, chunk, False).start()

        @pl.when(over < nshard)
        def _():
            basis_copy(1, over, chunk, False).wait_recv()

            @pl.when(shard > 0)
            def _():
                basis_copy(1, over, chunk, False).start()

    per = LANES // width
    if per > 1:
        for piece in range(nsplit * nshard):
            rows[piece // per, :, (piece % per) * width : (piece % per + 1) * width] = parts[piece // nshard, piece % nshard]

    else:
        rows[...] = parts[...].reshape(rows.shape)
    lane = lax.broadcasted_iota(jnp.int32, (LANES, LANES), 1)
    line = lax.broadcasted_iota(jnp.int32, (LANES, LANES), 0)
    mirror = jnp.where(lane + line == LANES - 1, 1.0, 0.0).astype(jnp.bfloat16)
    rows[...] = jnp.dot(
        rows[...].reshape(nrows * 8, LANES).astype(jnp.bfloat16), mirror,
        preferred_element_type=jnp.float32).reshape(rows.shape)

    def rolled(b):
        block = rows[b]
        return tuple(
            pltpu.roll(jnp.broadcast_to(block[d : d + 1, :], (LANES, LANES)), 0, 1, stride=1, stride_axis=0)
            for d in range(ndet))

    def tile_step(group, last):
        for i in range(4):
            b = group * 4 + i
            now = rolled(jnp.minimum(b + 1, nrows - 1))
            at = pl.ds(pl.multiple_of(b * LANES, LANES), LANES)
            for d in range(ndet):
                tiles[d, at, :] = jnp.where(lane >= line, last[d], now[d]).astype(jnp.bfloat16)
            last = now
        return last

    lax.fori_loop(0, nrows // 4, tile_step, rolled(jnp.int32(0)))

    @pl.loop(0, chunks)
    def _(step):
        advance(step)

    def place(first, second, chunk):
        at_taps = pl.ds(pl.multiple_of(chunk * ctaps, ctaps), ctaps)
        pair[:nb, :] = held[first, :, at_taps]
        pair[pad : pad + nb, :] = held[second, :, at_taps]
        turned[at_taps, :] = pair[...].T

    def keep(det, at, first, second, total):
        series[det, at, pl.ds(pl.multiple_of(first * pad, pad), pad)] = total[:, :pad].astype(jnp.bfloat16)
        series[det, at, pl.ds(pl.multiple_of(second * pad, pad), pad)] = total[:, pad:].astype(jnp.bfloat16)

    per_det = tout // mtile

    def fir_whole(first, second, beside):
        @pl.loop(0, chunks)
        def _(chunk):
            place(first, second, chunk)

        @pl.loop(0, ndet * per_det)
        def _(step):
            det = step // per_det
            begin = lax.rem(step, per_det) * mtile
            frame = jnp.concatenate([
                tiles[det, pl.ds(pl.multiple_of(begin + (ktiles - 1 - i) * LANES, LANES), mtile), :]
                for i in range(ktiles)], axis=1)
            at = pl.ds(pl.multiple_of(begin, mtile), mtile)
            keep(det, at, first, second, jnp.dot(frame, turned[...], preferred_element_type=jnp.float32))
            beside(step)

    def fir_part(first, second, chunk):
        place(first, second, chunk)
        at_taps = pl.ds(pl.multiple_of(chunk * ctaps, ctaps), ctaps)

        @pl.loop(0, ndet * per_det)
        def _(step):
            det = step // per_det
            begin = lax.rem(step, per_det) * mtile
            frame = jnp.concatenate([
                tiles[det, pl.ds(pl.multiple_of(begin + (ktiles - 1 - i) * LANES - chunk * ctaps, LANES), mtile), :]
                for i in range(ctaps // LANES)], axis=1)
            at = pl.ds(pl.multiple_of(begin, mtile), mtile)
            total = jnp.dot(frame, turned[at_taps, :], preferred_element_type=jnp.float32)
            total = jnp.where(chunk > 0, acc[det, at, :], 0.0) + total

            @pl.when(chunk < chunks - 1)
            def _():
                acc[det, at, :] = total

            @pl.when(chunk == chunks - 1)
            def _():
                keep(det, at, first, second, total)

    both = jnp.minimum(shard, nshard - 1 - shard)
    upper = shard >= nshard // 2

    def single(hop):
        return jnp.where(upper, shard - 1 - hop, shard + 1 + hop)

    @pl.loop(0, nshard - 1)
    def _(hop):
        late = hop - both
        paired = (late < 0) | ((late < nshard - 1 - 2 * both) & (lax.rem(late + 2 * nshard, 2) == 0))
        first = jnp.where(late < 0, shard - 1 - hop, jnp.where(late == 0, shard, single(hop - 1)))
        second = jnp.where(late < 0, shard + 1 + hop, single(hop))
        by_chunk = jnp.logical_not(middle) & (hop == nshard - 2)

        @pl.when(jnp.logical_not(middle) & (hop > 0) & jnp.logical_not(by_chunk))
        def _():
            @pl.loop(0, chunks)
            def _(step):
                advance(hop * chunks + step)

        @pl.when(by_chunk)
        def _():
            @pl.loop(0, chunks)
            def _(chunk):
                @pl.when(hop > 0)
                def _():
                    advance(hop * chunks + chunk)

                fir_part(first, second, chunk)

        def beside(step):
            @pl.when(middle & (hop + 1 < nshard - 1) & (step < chunks))
            def _():
                advance((hop + 1) * chunks + step)

        @pl.when(paired & jnp.logical_not(by_chunk))
        def _():
            fir_whole(first, second, beside)

        @pl.when(jnp.logical_not(paired))
        def _():
            @pl.loop(0, chunks)
            def _(step):
                beside(step)

    rtile = 256

    @pl.loop(0, tout // rtile)
    def _(step):
        at = pl.ds(pl.multiple_of(step * rtile, rtile), rtile)
        total = None
        for det in range(ndet):
            z = lax.dot_general(
                weights[...], series[det, at, :], (((1,), (1,)), ((), ())), preferred_element_type=jnp.float32)
            z = z * z
            z = z[:templ] + z[templ:]
            total = z if total is None else total + z
        total = total * scale
        snr_ref[:, at] = total
        top = jnp.max(total, axis=0, keepdims=True)
        for i in range(rtile // LANES):
            localmax[pl.ds(step * (rtile // LANES) + i, 1), :] = top[:, i * LANES : (i + 1) * LANES]

    def smax_copy(off):
        return pltpu.make_async_remote_copy(
            src_ref=localmax, dst_ref=splitmax.at[off - 1],
            send_sem=smax_send.at[off - 1], recv_sem=smax_recv.at[off - 1],
            device_id={"split": lax.rem(split + off, nsplit)}, device_id_type=MESH)

    for off in range(1, nsplit):
        smax_copy(off).start()
    for off in range(1, nsplit):
        smax_copy(off).wait_recv()
    most = localmax[...]
    for off in range(1, nsplit):
        most = jnp.maximum(most, splitmax[off - 1])
    shardmax[nshard - 1] = most

    def hmax_copy(off):
        return pltpu.make_async_remote_copy(
            src_ref=shardmax.at[nshard - 1], dst_ref=shardmax.at[off - 1],
            send_sem=hmax_send.at[off - 1], recv_sem=hmax_recv.at[off - 1],
            device_id={"shard": lax.rem(shard + off, nshard)}, device_id_type=MESH)

    for off in range(1, nshard):
        hmax_copy(off).start()
    for off in range(1, nshard):
        hmax_copy(off).wait_recv()
    for off in range(1, nshard):
        most = jnp.maximum(most, shardmax[off - 1])
    loud_ref[...] = most

    for off in range(1, nshard):
        strain_copy(off).wait_send()
        hmax_copy(off).wait_send()
    for off in range(1, nsplit):
        wide_copy(off).wait_send()
        smax_copy(off).wait_send()

    @pl.loop(0, nshard * chunks)
    def _(step):
        block, chunk = step // chunks, lax.rem(step, chunks)

        @pl.when((block <= shard) & (shard < nshard - 1))
        def _():
            basis_copy(0, block, chunk, False).wait_send()

        @pl.when((block >= shard) & (shard > 0))
        def _():
            basis_copy(1, block, chunk, False).wait_send()


def per_device(nsplit, nshard, strain, basis, recon):
    ndet, width = strain.shape
    _, nb, taps = basis.shape
    templ = recon.shape[2]
    tout = width * nsplit * nshard - taps
    pad = -(-nb // LANES) * LANES
    chunks = 4
    mtile = 512
    vmem = pl.BlockSpec(memory_space=pltpu.VMEM)
    dma = pltpu.SemaphoreType.DMA
    snr, loud = pl.pallas_call(
        functools.partial(kernel, nsplit, nshard, nb, pad, chunks, mtile, 1.0 / (2.0 * ndet)),
        out_shape=(
            pltpu.VMEM((templ, tout), jnp.float32),
            jax.ShapeDtypeStruct((tout // LANES, LANES), jnp.float32),
        ),
        in_specs=[vmem] * 3,
        out_specs=(vmem, vmem),
        scratch_shapes=[
            pltpu.VMEM((nsplit, nshard, 8, width), jnp.float32),
            pltpu.VMEM(((taps + tout) // LANES, 8, LANES), jnp.float32),
            pltpu.VMEM((ndet, taps + tout, LANES), jnp.bfloat16),
            pltpu.VMEM((nshard, nb, taps), jnp.bfloat16),
            pltpu.VMEM((2 * pad, taps // chunks), jnp.bfloat16),
            pltpu.VMEM((taps, 2 * pad), jnp.bfloat16),
            pltpu.VMEM((ndet, tout, 2 * pad), jnp.float32),
            pltpu.VMEM((ndet, tout, nshard * pad), jnp.bfloat16),
            pltpu.VMEM((2 * templ, nshard * pad), jnp.bfloat16),
            pltpu.VMEM((tout // LANES, LANES), jnp.float32),
            pltpu.VMEM((nsplit - 1, tout // LANES, LANES), jnp.float32),
            pltpu.VMEM((nshard, tout // LANES, LANES), jnp.float32),
            dma((nshard - 1,)), dma((nshard - 1,)),
            dma((nsplit - 1,)), dma((nsplit - 1,)),
            dma((2, nshard, chunks)), dma((nshard, chunks)),
            dma((nsplit - 1,)), dma((nsplit - 1,)),
            dma((nshard - 1,)), dma((nshard - 1,)),
        ],
        compiler_params=pltpu.CompilerParams(
            collective_id=0, has_side_effects=True, vmem_limit_bytes=56 * 1024 * 1024),
    )(strain, basis[0], jnp.swapaxes(recon[0], 1, 2))
    return snr[None], loud.reshape(tout)


def solution(mesh):
    return jax.shard_map(
        functools.partial(per_device, mesh.shape["split"], mesh.shape["shard"]),
        mesh=mesh,
        in_specs=(
            P(None, ("split", "shard")),
            P("split", "shard", None),
            P("split", None, "shard", None),
        ),
        out_specs=(P("split", "shard", None), P()),
        check_vma=False,
    )
```

```python
import functools

import jax
import jax.numpy as jnp
from jax import lax
from jax.experimental import pallas as pl
from jax.experimental.pallas import tpu as pltpu
from jax.sharding import PartitionSpec as P

MESH = pl.DeviceIdType.MESH
LANES = 128


def kernel(
    nsplit, nshard, nb, pad, chunks, mtile, scale,
    strain_ref, basis_ref, recon_ref,
    snr_ref, loud_ref,
    parts, rows, tiles, held, pair, turned, acc, series, weights, localmax, splitmax, shardmax,
    strain_send, strain_recv, wide_send, wide_recv,
    basis_send, basis_recv, smax_send, smax_recv, hmax_send, hmax_recv,
):
    split = lax.axis_index("split")
    shard = lax.axis_index("shard")
    ndet, width = strain_ref.shape
    taps = basis_ref.shape[1]
    tout = snr_ref.shape[1]
    templ = snr_ref.shape[0]
    ctaps = taps // chunks
    ktiles = taps // LANES
    nrows = (taps + tout) // LANES

    barrier = pltpu.get_barrier_semaphore()
    for off in range(1, nshard):
        pl.semaphore_signal(barrier, inc=1, device_id={"shard": lax.rem(shard + off, nshard)}, device_id_type=MESH)
    for off in range(1, nsplit):
        pl.semaphore_signal(barrier, inc=1, device_id={"split": lax.rem(split + off, nsplit)}, device_id_type=MESH)
    pl.semaphore_wait(barrier, nshard + nsplit - 2)

    parts[split, shard] = jnp.zeros((8, width), jnp.float32)
    parts[split, shard, :ndet] = strain_ref[...].astype(jnp.float32)

    def strain_copy(off):
        return pltpu.make_async_remote_copy(
            src_ref=parts.at[split, shard], dst_ref=parts.at[split, shard],
            send_sem=strain_send.at[off - 1], recv_sem=strain_recv.at[off - 1],
            device_id={"shard": lax.rem(shard + off, nshard)}, device_id_type=MESH)

    def wide_copy(off):
        return pltpu.make_async_remote_copy(
            src_ref=parts.at[split], dst_ref=parts.at[split],
            send_sem=wide_send.at[off - 1], recv_sem=wide_recv.at[off - 1],
            device_id={"split": lax.rem(split + off, nsplit)}, device_id_type=MESH)

    for off in range(1, nshard):
        strain_copy(off).start()

    def chunk_of(ref, chunk):
        return ref.at[:, pl.ds(pl.multiple_of(chunk * ctaps, ctaps), ctaps)]

    def basis_copy(way, block, chunk, own):
        dst = chunk_of(held.at[block], chunk)
        src = chunk_of(basis_ref, chunk) if own else dst
        target = shard + 1 if way == 0 else shard - 1
        return pltpu.make_async_remote_copy(
            src_ref=src, dst_ref=dst,
            send_sem=basis_send.at[way, block, chunk], recv_sem=basis_recv.at[block, chunk],
            device_id={"shard": target}, device_id_type=MESH)

    for chunk in range(chunks):
        @pl.when(shard < nshard - 1)
        def _():
            basis_copy(0, shard, chunk, True).start()

        @pl.when(shard > 0)
        def _():
            basis_copy(1, shard, chunk, True).start()

    held[shard] = basis_ref[...]
    lrow = lax.broadcasted_iota(jnp.int32, (nb * nshard, pad * nshard), 0)
    lcol = lax.broadcasted_iota(jnp.int32, (nb * nshard, pad * nshard), 1)
    within = lax.rem(lcol, pad)
    chosen = (lrow == (lcol - within) // pad * nb + within) & (within < nb)
    select = jnp.where(chosen, 1.0, 0.0).astype(jnp.bfloat16)

    def place_weights(q):
        @pl.loop(0, templ // 256)
        def _(part):
            begin = pl.multiple_of(part * 256, 256)
            placed = lax.dot_general(
                recon_ref[q, :, pl.ds(begin, 256)], select, (((0,), (0,)), ((), ())),
                preferred_element_type=jnp.float32)
            weights[pl.ds(pl.multiple_of(q * templ + begin, 256), 256), :] = placed.astype(jnp.bfloat16)

    place_weights(0)
    pair[...] = jnp.zeros_like(pair)

    for off in range(1, nshard):
        strain_copy(off).wait_recv()
    for off in range(1, nsplit):
        wide_copy(off).start()

    place_weights(1)
    for off in range(1, nsplit):
        wide_copy(off).wait_recv()

    middle = (shard > 0) & (shard < nshard - 1)

    def advance(step):
        hop, chunk = step // chunks, lax.rem(step, chunks)
        below, over = shard - 1 - hop, shard + 1 + hop

        @pl.when(below >= 0)
        def _():
            basis_copy(0, below, chunk, False).wait_recv()

            @pl.when(shard < nshard - 1)
            def _():
                basis_copy(0, below, chunk, False).start()

        @pl.when(over < nshard)
        def _():
            basis_copy(1, over, chunk, False).wait_recv()

            @pl.when(shard > 0)
            def _():
                basis_copy(1, over, chunk, False).start()

    ahead = min(2, chunks)

    @pl.when(middle)
    def _():
        for step in range(ahead):
            advance(jnp.int32(step))

    per = LANES // width
    if per > 1:
        for piece in range(nsplit * nshard):
            rows[piece // per, :, (piece % per) * width : (piece % per + 1) * width] = parts[piece // nshard, piece % nshard]

    else:
        rows[...] = parts[...].reshape(rows.shape)
    lane = lax.broadcasted_iota(jnp.int32, (LANES, LANES), 1)
    line = lax.broadcasted_iota(jnp.int32, (LANES, LANES), 0)
    mirror = jnp.where(lane + line == LANES - 1, 1.0, 0.0).astype(jnp.bfloat16)
    rows[...] = jnp.dot(
        rows[...].reshape(nrows * 8, LANES).astype(jnp.bfloat16), mirror,
        preferred_element_type=jnp.float32).reshape(rows.shape)

    def rolled(b):
        block = rows[b]
        return tuple(
            pltpu.roll(jnp.broadcast_to(block[d : d + 1, :], (LANES, LANES)), 0, 1, stride=1, stride_axis=0)
            for d in range(ndet))

    def tile_step(group, last):
        for i in range(4):
            b = group * 4 + i
            now = rolled(jnp.minimum(b + 1, nrows - 1))
            at = pl.ds(pl.multiple_of(b * LANES, LANES), LANES)
            for d in range(ndet):
                tiles[d, at, :] = jnp.where(lane >= line, last[d], now[d]).astype(jnp.bfloat16)
            last = now
        return last

    lax.fori_loop(0, nrows // 4, tile_step, rolled(jnp.int32(0)))

    @pl.loop(jnp.where(middle, ahead, 0), chunks)
    def _(step):
        advance(step)

    def place(first, second, chunk):
        at_taps = pl.ds(pl.multiple_of(chunk * ctaps, ctaps), ctaps)
        pair[:nb, :] = held[first, :, at_taps]
        pair[pad : pad + nb, :] = held[second, :, at_taps]
        turned[at_taps, :] = pair[...].T

    def keep(det, at, first, second, total):
        series[det, at, pl.ds(pl.multiple_of(first * pad, pad), pad)] = total[:, :pad].astype(jnp.bfloat16)
        series[det, at, pl.ds(pl.multiple_of(second * pad, pad), pad)] = total[:, pad:].astype(jnp.bfloat16)

    per_det = tout // mtile

    def fir_whole(first, second, beside):
        @pl.loop(0, chunks)
        def _(chunk):
            place(first, second, chunk)

        @pl.loop(0, ndet * per_det)
        def _(step):
            det = step // per_det
            begin = lax.rem(step, per_det) * mtile
            frame = jnp.concatenate([
                tiles[det, pl.ds(pl.multiple_of(begin + (ktiles - 1 - i) * LANES, LANES), mtile), :]
                for i in range(ktiles)], axis=1)
            at = pl.ds(pl.multiple_of(begin, mtile), mtile)
            keep(det, at, first, second, jnp.dot(frame, turned[...], preferred_element_type=jnp.float32))
            beside(step)

    def fir_part(first, second, chunk):
        place(first, second, chunk)
        at_taps = pl.ds(pl.multiple_of(chunk * ctaps, ctaps), ctaps)

        @pl.loop(0, ndet * per_det)
        def _(step):
            det = step // per_det
            begin = lax.rem(step, per_det) * mtile
            frame = jnp.concatenate([
                tiles[det, pl.ds(pl.multiple_of(begin + (ktiles - 1 - i) * LANES - chunk * ctaps, LANES), mtile), :]
                for i in range(ctaps // LANES)], axis=1)
            at = pl.ds(pl.multiple_of(begin, mtile), mtile)
            total = jnp.dot(frame, turned[at_taps, :], preferred_element_type=jnp.float32)
            total = jnp.where(chunk > 0, acc[det, at, :], 0.0) + total

            @pl.when(chunk < chunks - 1)
            def _():
                acc[det, at, :] = total

            @pl.when(chunk == chunks - 1)
            def _():
                keep(det, at, first, second, total)

    both = jnp.minimum(shard, nshard - 1 - shard)
    upper = shard >= nshard // 2

    def single(hop):
        return jnp.where(upper, shard - 1 - hop, shard + 1 + hop)

    @pl.loop(0, nshard - 1)
    def _(hop):
        late = hop - both
        paired = (late < 0) | ((late < nshard - 1 - 2 * both) & (lax.rem(late + 2 * nshard, 2) == 0))
        first = jnp.where(late < 0, shard - 1 - hop, jnp.where(late == 0, shard, single(hop - 1)))
        second = jnp.where(late < 0, shard + 1 + hop, single(hop))
        by_chunk = jnp.logical_not(middle) & (hop == nshard - 2)

        @pl.when(jnp.logical_not(middle) & (hop > 0) & jnp.logical_not(by_chunk))
        def _():
            @pl.loop(0, chunks)
            def _(step):
                advance(hop * chunks + step)

        @pl.when(by_chunk)
        def _():
            @pl.loop(0, chunks)
            def _(chunk):
                @pl.when(hop > 0)
                def _():
                    advance(hop * chunks + chunk)

                fir_part(first, second, chunk)

        def beside(step):
            @pl.when(middle & (hop + 1 < nshard - 1) & (step < chunks))
            def _():
                advance((hop + 1) * chunks + step)

        @pl.when(paired & jnp.logical_not(by_chunk))
        def _():
            fir_whole(first, second, beside)

        @pl.when(jnp.logical_not(paired))
        def _():
            @pl.loop(0, chunks)
            def _(step):
                beside(step)

    rtile = 256

    @pl.loop(0, tout // rtile)
    def _(step):
        at = pl.ds(pl.multiple_of(step * rtile, rtile), rtile)
        total = None
        for det in range(ndet):
            z = lax.dot_general(
                weights[...], series[det, at, :], (((1,), (1,)), ((), ())), preferred_element_type=jnp.float32)
            z = z * z
            z = z[:templ] + z[templ:]
            total = z if total is None else total + z
        total = total * scale
        snr_ref[:, at] = total
        top = jnp.max(total, axis=0, keepdims=True)
        for i in range(rtile // LANES):
            localmax[pl.ds(step * (rtile // LANES) + i, 1), :] = top[:, i * LANES : (i + 1) * LANES]

    def smax_copy(off):
        return pltpu.make_async_remote_copy(
            src_ref=localmax, dst_ref=splitmax.at[off - 1],
            send_sem=smax_send.at[off - 1], recv_sem=smax_recv.at[off - 1],
            device_id={"split": lax.rem(split + off, nsplit)}, device_id_type=MESH)

    for off in range(1, nsplit):
        smax_copy(off).start()
    for off in range(1, nsplit):
        smax_copy(off).wait_recv()
    most = localmax[...]
    for off in range(1, nsplit):
        most = jnp.maximum(most, splitmax[off - 1])
    shardmax[nshard - 1] = most

    def hmax_copy(off):
        return pltpu.make_async_remote_copy(
            src_ref=shardmax.at[nshard - 1], dst_ref=shardmax.at[off - 1],
            send_sem=hmax_send.at[off - 1], recv_sem=hmax_recv.at[off - 1],
            device_id={"shard": lax.rem(shard + off, nshard)}, device_id_type=MESH)

    for off in range(1, nshard):
        hmax_copy(off).start()
    for off in range(1, nshard):
        hmax_copy(off).wait_recv()
    for off in range(1, nshard):
        most = jnp.maximum(most, shardmax[off - 1])
    loud_ref[...] = most

    for off in range(1, nshard):
        strain_copy(off).wait_send()
        hmax_copy(off).wait_send()
    for off in range(1, nsplit):
        wide_copy(off).wait_send()
        smax_copy(off).wait_send()

    @pl.loop(0, nshard * chunks)
    def _(step):
        block, chunk = step // chunks, lax.rem(step, chunks)

        @pl.when((block <= shard) & (shard < nshard - 1))
        def _():
            basis_copy(0, block, chunk, False).wait_send()

        @pl.when((block >= shard) & (shard > 0))
        def _():
            basis_copy(1, block, chunk, False).wait_send()


def per_device(nsplit, nshard, strain, basis, recon):
    ndet, width = strain.shape
    _, nb, taps = basis.shape
    templ = recon.shape[2]
    tout = width * nsplit * nshard - taps
    pad = -(-nb // LANES) * LANES
    chunks = 4
    mtile = 1024
    vmem = pl.BlockSpec(memory_space=pltpu.VMEM)
    dma = pltpu.SemaphoreType.DMA
    snr, loud = pl.pallas_call(
        functools.partial(kernel, nsplit, nshard, nb, pad, chunks, mtile, 1.0 / (2.0 * ndet)),
        out_shape=(
            pltpu.VMEM((templ, tout), jnp.float32),
            jax.ShapeDtypeStruct((tout // LANES, LANES), jnp.float32),
        ),
        in_specs=[vmem] * 3,
        out_specs=(vmem, vmem),
        scratch_shapes=[
            pltpu.VMEM((nsplit, nshard, 8, width), jnp.float32),
            pltpu.VMEM(((taps + tout) // LANES, 8, LANES), jnp.float32),
            pltpu.VMEM((ndet, taps + tout, LANES), jnp.bfloat16),
            pltpu.VMEM((nshard, nb, taps), jnp.bfloat16),
            pltpu.VMEM((2 * pad, taps // chunks), jnp.bfloat16),
            pltpu.VMEM((taps, 2 * pad), jnp.bfloat16),
            pltpu.VMEM((ndet, tout, 2 * pad), jnp.float32),
            pltpu.VMEM((ndet, tout, nshard * pad), jnp.bfloat16),
            pltpu.VMEM((2 * templ, nshard * pad), jnp.bfloat16),
            pltpu.VMEM((tout // LANES, LANES), jnp.float32),
            pltpu.VMEM((nsplit - 1, tout // LANES, LANES), jnp.float32),
            pltpu.VMEM((nshard, tout // LANES, LANES), jnp.float32),
            dma((nshard - 1,)), dma((nshard - 1,)),
            dma((nsplit - 1,)), dma((nsplit - 1,)),
            dma((2, nshard, chunks)), dma((nshard, chunks)),
            dma((nsplit - 1,)), dma((nsplit - 1,)),
            dma((nshard - 1,)), dma((nshard - 1,)),
        ],
        compiler_params=pltpu.CompilerParams(
            collective_id=0, has_side_effects=True, vmem_limit_bytes=56 * 1024 * 1024),
    )(strain, basis[0], jnp.swapaxes(recon[0], 1, 2))
    return snr[None], loud.reshape(tout)


def solution(mesh):
    return jax.shard_map(
        functools.partial(per_device, mesh.shape["split"], mesh.shape["shard"]),
        mesh=mesh,
        in_specs=(
            P(None, ("split", "shard")),
            P("split", "shard", None),
            P("split", None, "shard", None),
        ),
        out_specs=(P("split", "shard", None), P()),
        check_vma=False,
    )
```

```python
import functools

import jax
import jax.numpy as jnp
from jax import lax
from jax.experimental import pallas as pl
from jax.experimental.pallas import tpu as pltpu
from jax.sharding import PartitionSpec as P

MESH = pl.DeviceIdType.MESH
LANES = 128


def kernel(
    nsplit, nshard, nb, pad, chunks, mtile, scale,
    strain_ref, basis_ref, recon_ref,
    snr_ref, loud_ref,
    parts, rows, tiles, held, pair, turned, acc, series, weights, localmax, splitmax, shardmax,
    strain_send, strain_recv, wide_send, wide_recv,
    basis_send, basis_recv, smax_send, smax_recv, hmax_send, hmax_recv,
):
    split = lax.axis_index("split")
    shard = lax.axis_index("shard")
    ndet, width = strain_ref.shape
    taps = basis_ref.shape[1]
    tout = snr_ref.shape[1]
    templ = snr_ref.shape[0]
    ctaps = taps // chunks
    ktiles = taps // LANES
    nrows = (taps + tout) // LANES

    barrier = pltpu.get_barrier_semaphore()
    for off in range(1, nshard):
        pl.semaphore_signal(barrier, inc=1, device_id={"shard": lax.rem(shard + off, nshard)}, device_id_type=MESH)
    for off in range(1, nsplit):
        pl.semaphore_signal(barrier, inc=1, device_id={"split": lax.rem(split + off, nsplit)}, device_id_type=MESH)
    pl.semaphore_wait(barrier, nshard + nsplit - 2)

    parts[split, shard] = jnp.zeros((8, width), jnp.float32)
    parts[split, shard, :ndet] = strain_ref[...].astype(jnp.float32)

    def strain_copy(off):
        return pltpu.make_async_remote_copy(
            src_ref=parts.at[split, shard], dst_ref=parts.at[split, shard],
            send_sem=strain_send.at[off - 1], recv_sem=strain_recv.at[off - 1],
            device_id={"shard": lax.rem(shard + off, nshard)}, device_id_type=MESH)

    def wide_copy(off):
        return pltpu.make_async_remote_copy(
            src_ref=parts.at[split], dst_ref=parts.at[split],
            send_sem=wide_send.at[off - 1], recv_sem=wide_recv.at[off - 1],
            device_id={"split": lax.rem(split + off, nsplit)}, device_id_type=MESH)

    for off in range(1, nshard):
        strain_copy(off).start()

    def chunk_of(ref, chunk):
        return ref.at[:, pl.ds(pl.multiple_of(chunk * ctaps, ctaps), ctaps)]

    def basis_copy(way, block, chunk, own):
        dst = chunk_of(held.at[block], chunk)
        src = chunk_of(basis_ref, chunk) if own else dst
        target = shard + 1 if way == 0 else shard - 1
        return pltpu.make_async_remote_copy(
            src_ref=src, dst_ref=dst,
            send_sem=basis_send.at[way, block, chunk], recv_sem=basis_recv.at[block, chunk],
            device_id={"shard": target}, device_id_type=MESH)

    for chunk in range(chunks):
        @pl.when(shard < nshard - 1)
        def _():
            basis_copy(0, shard, chunk, True).start()

        @pl.when(shard > 0)
        def _():
            basis_copy(1, shard, chunk, True).start()

    held[shard] = basis_ref[...]
    lrow = lax.broadcasted_iota(jnp.int32, (nb * nshard, pad * nshard), 0)
    lcol = lax.broadcasted_iota(jnp.int32, (nb * nshard, pad * nshard), 1)
    within = lax.rem(lcol, pad)
    chosen = (lrow == (lcol - within) // pad * nb + within) & (within < nb)
    select = jnp.where(chosen, 1.0, 0.0).astype(jnp.bfloat16)

    def place_weights(q):
        @pl.loop(0, templ // 256)
        def _(part):
            begin = pl.multiple_of(part * 256, 256)
            placed = lax.dot_general(
                recon_ref[q, :, pl.ds(begin, 256)], select, (((0,), (0,)), ((), ())),
                preferred_element_type=jnp.float32)
            weights[pl.ds(pl.multiple_of(q * templ + begin, 256), 256), :] = placed.astype(jnp.bfloat16)

    place_weights(0)
    pair[...] = jnp.zeros_like(pair)

    for off in range(1, nshard):
        strain_copy(off).wait_recv()
    for off in range(1, nsplit):
        wide_copy(off).start()

    place_weights(1)
    for off in range(1, nsplit):
        wide_copy(off).wait_recv()

    middle = (shard > 0) & (shard < nshard - 1)

    def advance(step):
        hop, chunk = step // chunks, lax.rem(step, chunks)
        below, over = shard - 1 - hop, shard + 1 + hop

        @pl.when(below >= 0)
        def _():
            basis_copy(0, below, chunk, False).wait_recv()

            @pl.when(shard < nshard - 1)
            def _():
                basis_copy(0, below, chunk, False).start()

        @pl.when(over < nshard)
        def _():
            basis_copy(1, over, chunk, False).wait_recv()

            @pl.when(shard > 0)
            def _():
                basis_copy(1, over, chunk, False).start()

    ahead = min(2, chunks)

    @pl.when(middle)
    def _():
        for step in range(ahead):
            advance(jnp.int32(step))

    per = LANES // width
    if per > 1:
        for piece in range(nsplit * nshard):
            rows[piece // per, :, (piece % per) * width : (piece % per + 1) * width] = parts[piece // nshard, piece % nshard]

    else:
        rows[...] = parts[...].reshape(rows.shape)
    lane = lax.broadcasted_iota(jnp.int32, (LANES, LANES), 1)
    line = lax.broadcasted_iota(jnp.int32, (LANES, LANES), 0)
    mirror = jnp.where(lane + line == LANES - 1, 1.0, 0.0).astype(jnp.bfloat16)
    rows[...] = jnp.dot(
        rows[...].reshape(nrows * 8, LANES).astype(jnp.bfloat16), mirror,
        preferred_element_type=jnp.float32).reshape(rows.shape)

    def rolled(b):
        block = rows[b]
        return tuple(
            pltpu.roll(jnp.broadcast_to(block[d : d + 1, :], (LANES, LANES)), 0, 1, stride=1, stride_axis=0)
            for d in range(ndet))

    def tile_step(group, last):
        for i in range(4):
            b = group * 4 + i
            now = rolled(jnp.minimum(b + 1, nrows - 1))
            at = pl.ds(pl.multiple_of(b * LANES, LANES), LANES)
            for d in range(ndet):
                tiles[d, at, :] = jnp.where(lane >= line, last[d], now[d]).astype(jnp.bfloat16)
            last = now
        return last

    lax.fori_loop(0, nrows // 4, tile_step, rolled(jnp.int32(0)))

    @pl.loop(jnp.where(middle, ahead, 0), chunks)
    def _(step):
        advance(step)

    def place(first, second, chunk):
        at_taps = pl.ds(pl.multiple_of(chunk * ctaps, ctaps), ctaps)
        pair[:nb, :] = held[first, :, at_taps]
        pair[pad : pad + nb, :] = held[second, :, at_taps]
        turned[at_taps, :] = pair[...].T

    def keep(det, at, first, second, total):
        series[det, at, pl.ds(pl.multiple_of(first * pad, pad), pad)] = total[:, :pad].astype(jnp.bfloat16)
        series[det, at, pl.ds(pl.multiple_of(second * pad, pad), pad)] = total[:, pad:].astype(jnp.bfloat16)

    per_det = tout // mtile

    wtile = min(2 * mtile, tout)
    per_whole = tout // wtile
    span = -(-chunks // (ndet * per_whole))

    def fir_whole(first, second, beside):
        @pl.loop(0, chunks)
        def _(chunk):
            place(first, second, chunk)

        @pl.loop(0, ndet * per_whole)
        def _(step):
            det = step // per_whole
            begin = lax.rem(step, per_whole) * wtile
            frame = jnp.concatenate([
                tiles[det, pl.ds(pl.multiple_of(begin + (ktiles - 1 - i) * LANES, LANES), wtile), :]
                for i in range(ktiles)], axis=1)
            at = pl.ds(pl.multiple_of(begin, wtile), wtile)
            keep(det, at, first, second, jnp.dot(frame, turned[...], preferred_element_type=jnp.float32))
            for i in range(span):
                beside(step * span + i)

    def fir_part(first, second, chunk):
        place(first, second, chunk)
        at_taps = pl.ds(pl.multiple_of(chunk * ctaps, ctaps), ctaps)

        @pl.loop(0, ndet * per_det)
        def _(step):
            det = step // per_det
            begin = lax.rem(step, per_det) * mtile
            frame = jnp.concatenate([
                tiles[det, pl.ds(pl.multiple_of(begin + (ktiles - 1 - i) * LANES - chunk * ctaps, LANES), mtile), :]
                for i in range(ctaps // LANES)], axis=1)
            at = pl.ds(pl.multiple_of(begin, mtile), mtile)
            total = jnp.dot(frame, turned[at_taps, :], preferred_element_type=jnp.float32)
            total = jnp.where(chunk > 0, acc[det, at, :], 0.0) + total

            @pl.when(chunk < chunks - 1)
            def _():
                acc[det, at, :] = total

            @pl.when(chunk == chunks - 1)
            def _():
                keep(det, at, first, second, total)

    both = jnp.minimum(shard, nshard - 1 - shard)
    upper = shard >= nshard // 2

    def single(hop):
        return jnp.where(upper, shard - 1 - hop, shard + 1 + hop)

    @pl.loop(0, nshard - 1)
    def _(hop):
        late = hop - both
        paired = (late < 0) | ((late < nshard - 1 - 2 * both) & (lax.rem(late + 2 * nshard, 2) == 0))
        first = jnp.where(late < 0, shard - 1 - hop, jnp.where(late == 0, shard, single(hop - 1)))
        second = jnp.where(late < 0, shard + 1 + hop, single(hop))
        by_chunk = jnp.logical_not(middle) & (hop == nshard - 2)

        @pl.when(jnp.logical_not(middle) & (hop > 0) & jnp.logical_not(by_chunk))
        def _():
            @pl.loop(0, chunks)
            def _(step):
                advance(hop * chunks + step)

        @pl.when(by_chunk)
        def _():
            @pl.loop(0, chunks)
            def _(chunk):
                @pl.when(hop > 0)
                def _():
                    advance(hop * chunks + chunk)

                fir_part(first, second, chunk)

        def beside(step):
            @pl.when(middle & (hop + 1 < nshard - 1) & (step < chunks))
            def _():
                advance((hop + 1) * chunks + step)

        @pl.when(paired & jnp.logical_not(by_chunk))
        def _():
            fir_whole(first, second, beside)

        @pl.when(jnp.logical_not(paired))
        def _():
            @pl.loop(0, chunks)
            def _(step):
                beside(step)

    rtile = 256

    @pl.loop(0, tout // rtile)
    def _(step):
        at = pl.ds(pl.multiple_of(step * rtile, rtile), rtile)
        total = None
        for det in range(ndet):
            z = lax.dot_general(
                weights[...], series[det, at, :], (((1,), (1,)), ((), ())), preferred_element_type=jnp.float32)
            z = z * z
            z = z[:templ] + z[templ:]
            total = z if total is None else total + z
        total = total * scale
        snr_ref[:, at] = total
        top = jnp.max(total, axis=0, keepdims=True)
        for i in range(rtile // LANES):
            localmax[pl.ds(step * (rtile // LANES) + i, 1), :] = top[:, i * LANES : (i + 1) * LANES]

    def smax_copy(off):
        return pltpu.make_async_remote_copy(
            src_ref=localmax, dst_ref=splitmax.at[off - 1],
            send_sem=smax_send.at[off - 1], recv_sem=smax_recv.at[off - 1],
            device_id={"split": lax.rem(split + off, nsplit)}, device_id_type=MESH)

    for off in range(1, nsplit):
        smax_copy(off).start()
    for off in range(1, nsplit):
        smax_copy(off).wait_recv()
    most = localmax[...]
    for off in range(1, nsplit):
        most = jnp.maximum(most, splitmax[off - 1])
    shardmax[nshard - 1] = most

    def hmax_copy(off):
        return pltpu.make_async_remote_copy(
            src_ref=shardmax.at[nshard - 1], dst_ref=shardmax.at[off - 1],
            send_sem=hmax_send.at[off - 1], recv_sem=hmax_recv.at[off - 1],
            device_id={"shard": lax.rem(shard + off, nshard)}, device_id_type=MESH)

    for off in range(1, nshard):
        hmax_copy(off).start()
    for off in range(1, nshard):
        hmax_copy(off).wait_recv()
    for off in range(1, nshard):
        most = jnp.maximum(most, shardmax[off - 1])
    loud_ref[...] = most

    for off in range(1, nshard):
        strain_copy(off).wait_send()
        hmax_copy(off).wait_send()
    for off in range(1, nsplit):
        wide_copy(off).wait_send()
        smax_copy(off).wait_send()

    @pl.loop(0, nshard * chunks)
    def _(step):
        block, chunk = step // chunks, lax.rem(step, chunks)

        @pl.when((block <= shard) & (shard < nshard - 1))
        def _():
            basis_copy(0, block, chunk, False).wait_send()

        @pl.when((block >= shard) & (shard > 0))
        def _():
            basis_copy(1, block, chunk, False).wait_send()


def per_device(nsplit, nshard, strain, basis, recon):
    ndet, width = strain.shape
    _, nb, taps = basis.shape
    templ = recon.shape[2]
    tout = width * nsplit * nshard - taps
    pad = -(-nb // LANES) * LANES
    chunks = 4
    mtile = 1024
    vmem = pl.BlockSpec(memory_space=pltpu.VMEM)
    dma = pltpu.SemaphoreType.DMA
    snr, loud = pl.pallas_call(
        functools.partial(kernel, nsplit, nshard, nb, pad, chunks, mtile, 1.0 / (2.0 * ndet)),
        out_shape=(
            pltpu.VMEM((templ, tout), jnp.float32),
            jax.ShapeDtypeStruct((tout // LANES, LANES), jnp.float32),
        ),
        in_specs=[vmem] * 3,
        out_specs=(vmem, vmem),
        scratch_shapes=[
            pltpu.VMEM((nsplit, nshard, 8, width), jnp.float32),
            pltpu.VMEM(((taps + tout) // LANES, 8, LANES), jnp.float32),
            pltpu.VMEM((ndet, taps + tout, LANES), jnp.bfloat16),
            pltpu.VMEM((nshard, nb, taps), jnp.bfloat16),
            pltpu.VMEM((2 * pad, taps // chunks), jnp.bfloat16),
            pltpu.VMEM((taps, 2 * pad), jnp.bfloat16),
            pltpu.VMEM((ndet, tout, 2 * pad), jnp.float32),
            pltpu.VMEM((ndet, tout, nshard * pad), jnp.bfloat16),
            pltpu.VMEM((2 * templ, nshard * pad), jnp.bfloat16),
            pltpu.VMEM((tout // LANES, LANES), jnp.float32),
            pltpu.VMEM((nsplit - 1, tout // LANES, LANES), jnp.float32),
            pltpu.VMEM((nshard, tout // LANES, LANES), jnp.float32),
            dma((nshard - 1,)), dma((nshard - 1,)),
            dma((nsplit - 1,)), dma((nsplit - 1,)),
            dma((2, nshard, chunks)), dma((nshard, chunks)),
            dma((nsplit - 1,)), dma((nsplit - 1,)),
            dma((nshard - 1,)), dma((nshard - 1,)),
        ],
        compiler_params=pltpu.CompilerParams(
            collective_id=0, has_side_effects=True, vmem_limit_bytes=56 * 1024 * 1024),
    )(strain, basis[0], jnp.swapaxes(recon[0], 1, 2))
    return snr[None], loud.reshape(tout)


def solution(mesh):
    return jax.shard_map(
        functools.partial(per_device, mesh.shape["split"], mesh.shape["shard"]),
        mesh=mesh,
        in_specs=(
            P(None, ("split", "shard")),
            P("split", "shard", None),
            P("split", None, "shard", None),
        ),
        out_specs=(P("split", "shard", None), P()),
        check_vma=False,
    )
```
